32 devices in a mesh: dp: 8 (over z, core), tensor: 4 (over y, x).
Axes of the slice: x: 2, y: 2, z: 4, core: 2. Of those that a mesh axis runs over, the one named last changes fastest.
Arguments:
- grad_query: bfloat16 [2048, 8192], P('dp', 'tensor'), may hold values from -6 to 6
- query_weight: bfloat16 [8192, 8192], P('dp', 'tensor')
- grad_resid: bfloat16 [2048, 8192], P('dp', 'tensor'), may hold values from -6 to 6
- embeds: bfloat16 [2048, 8192], P('dp', 'tensor')
- norm_gain: float32 [8192], P('tensor'), may hold values from 0.1 to 1.9
- img_pos: int32 [8, 128], P('dp'), may hold values from 0 to 255, as said below
- img_count: int32 [8], P('dp'), may hold values from 64 to 128, as said below
- img_dest: int32 [8, 128], P('dp'), may hold values from 0 to 7, as said below
- merge_weight: bfloat16 [5120, 8192], P('dp', 'tensor'), may hold values from -0.0625 to 0.0625
- merge_pre: bfloat16 [1536, 5120], P('dp', 'tensor'), may hold values from -5 to 5
Outputs:
- grad_pre: float32 [1536, 5120], P('dp', 'tensor')
The draws below stay inside these ranges and needn't reach their ends.
Inputs may be any that keep to these rules, and one draw needn't show every extreme that they name: `img_pos`: positions of one device are distinct. `img_count`: at least 64 on every device; some device has 128. `img_dest`: among the rows of one device no encoder device is named more than 24 times; the first 24 rows of every device name one common encoder device, which so receives 24 live rows from every device.
All inputs are finite; a program needn't handle non-finite values.
Results may differ from the reference program's by a relative error of at most 0.034.
Values may be sent and summed in bfloat16 or wider, within the bound.
A program may use at most 128 MiB of HBM per device.

```python
import math
import jax
import jax.numpy as jnp
from jax import lax

D = 8192
QW = 8192
MH = 5120
TOK_DEV = 256
IMG_MAX = 128
CAP = 24
ENC_DEV = 192
TOKENS = 2048
ENC_ROWS = 1536
N_DP = 8
N_TENSOR = 4


def shared_direction(key):
    return jax.random.normal(jax.random.fold_in(key, 5), (D,), jnp.float32)


def draw_query_weight(key, part):
    direction = shared_direction(key)
    key = jax.random.fold_in(key, 51)
    key_noise, key_along = jax.random.split(key)
    noise = jax.random.normal(key_noise, (D, QW), jnp.float32) * QW ** (-0.5)
    along = jax.random.normal(key_along, (QW,), jnp.float32) * QW ** (-0.5)
    return (noise + direction[:, None] * along[None, :]).astype(jnp.bfloat16)


def draw_embeds(key, part):
    direction = shared_direction(key)
    key = jax.random.fold_in(key, 11)
    key_base = jax.random.fold_in(key, 0)
    key_rows = jax.random.fold_in(key, 1)
    key_cols = jax.random.fold_in(key, 2)
    key_blocks = jax.random.fold_in(key, 4)
    key_along = jax.random.fold_in(key, 5)
    base = jax.random.normal(key_base, (TOKENS, D), jnp.float32)
    along = 1.2 * jax.random.normal(key_along, (TOKENS, 1), jnp.float32)
    base = base + along * direction[None, :]
    row_scale = jnp.exp(jax.random.uniform(key_rows, (TOKENS, 1), jnp.float32, math.log(0.3), math.log(3.0)))
    block_scale = jnp.exp(jax.random.uniform(key_blocks, (N_TENSOR,), jnp.float32, math.log(0.3), math.log(3.0)))
    col_scale = jnp.repeat(block_scale, D // N_TENSOR) * jnp.exp(jax.random.uniform(key_cols, (D,), jnp.float32, math.log(0.7), math.log(1.4)))
    return (base * row_scale * col_scale[None, :]).astype(jnp.bfloat16)


def draw_img_pos(key, part):
    key = jax.random.fold_in(key, 21)
    device_keys = jax.random.split(key, N_DP)
    return jax.vmap(lambda one_key: jax.random.permutation(one_key, TOK_DEV)[:IMG_MAX])(device_keys).astype(jnp.int32)


def draw_img_count(key, part):
    key = jax.random.fold_in(key, 31)
    key_counts, key_full = jax.random.split(key)
    counts = jax.random.randint(key_counts, (N_DP,), IMG_MAX // 2, IMG_MAX + 1)
    full_device = jax.random.randint(key_full, (), 0, N_DP)
    return jnp.where(jnp.arange(N_DP) == full_device, IMG_MAX, counts).astype(jnp.int32)


def draw_img_dest(key, part):
    key = jax.random.fold_in(key, 41)
    key_common, key_rows = jax.random.split(key)
    common_dev = jax.random.randint(key_common, (), 0, N_DP)
    slot_dev = jnp.arange(ENC_DEV, dtype=jnp.int32) // CAP

    def one_device(one_key):
        scores = jax.random.permutation(one_key, ENC_DEV).astype(jnp.int32)
        scores = jnp.where(slot_dev == common_dev, scores - ENC_DEV, scores)
        order = jnp.argsort(scores, stable=True)
        return slot_dev[order[:IMG_MAX]]
    return jax.vmap(one_device)(jax.random.split(key_rows, N_DP)).astype(jnp.int32)


def level_of(own_key, dims, shards, least, high):
    gain = 1.0
    for axis_at, blocks in shards:
        draws = jax.random.uniform(jax.random.fold_in(jax.random.fold_in(own_key, 6), axis_at), (blocks,), jnp.float32, least / len(shards), high / len(shards))
        gain = gain * jnp.repeat(jnp.exp(draws), dims[axis_at] // blocks).reshape((-1,) + (1,) * (len(dims) - 1 - axis_at))
    return gain


def gaussian(rng, shape, deviation, bound, cuts=(), kind=jnp.bfloat16):
    drawn = deviation * jax.random.normal(rng, shape, jnp.float32)
    if cuts:
        drawn = drawn * level_of(rng, shape, cuts, -0.22, 0.18)
    return jnp.clip(drawn, -bound, bound).astype(kind)


def setup_inputs(seed: int = 0) -> dict:
    key_list = jax.random.split(jax.random.key(seed), 11)
    return {
        "grad_query": gaussian(key_list[0], (TOKENS, QW), 1.0, 6.0, ((0, 8), (1, 4))),
        "query_weight": draw_query_weight(jax.random.fold_in(key_list[10], 71), 0),
        "grad_resid": gaussian(key_list[2], (TOKENS, D), 1.0, 6.0, ((0, 8), (1, 4))),
        "embeds": draw_embeds(jax.random.fold_in(key_list[10], 71), 0),
        "norm_gain": jnp.clip(1.0 + 0.18 * jax.random.normal(key_list[4], (D,), jnp.float32), 0.1, 1.9),
        "img_pos": draw_img_pos(jax.random.fold_in(key_list[10], 71), 0),
        "img_count": draw_img_count(jax.random.fold_in(key_list[10], 71), 0),
        "img_dest": draw_img_dest(jax.random.fold_in(key_list[10], 71), 0),
        "merge_weight": gaussian(key_list[8], (MH, D), D ** -0.5, 0.0625, ((0, 8), (1, 4))),
        "merge_pre": gaussian(key_list[9], (ENC_ROWS, MH), 1.0, 5.0, ((0, 8), (1, 4))),
    }


NORM_EPS = 1e-06

def gelu_slope(pre):
    value = pre.astype(jnp.float32)
    cdf_part = 0.5 * (1.0 + lax.erf(value * 0.7071067811865476))
    pdf_part = jnp.exp(-0.5 * value * value) * 0.3989422804014327
    return cdf_part + value * pdf_part

def reference(grad_query, query_weight, grad_resid, embeds, norm_gain, img_pos, img_count, img_dest, merge_weight, merge_pre):
    flat_rows = (jnp.arange(N_DP, dtype=jnp.int32)[:, None] * TOK_DEV + img_pos).reshape(-1)
    picked = jnp.take(grad_query, flat_rows, axis=0)
    query_local = QW // N_TENSOR
    normal_grad = jnp.zeros((N_DP * IMG_MAX, D), jnp.float32)
    for part_index in range(N_TENSOR):
        lower = part_index * query_local
        term = jnp.dot(picked[:, lower:lower + query_local], query_weight[:, lower:lower + query_local].T, preferred_element_type=jnp.float32)
        term = lax.optimization_barrier(term.astype(jnp.bfloat16))
        normal_grad = normal_grad + term.astype(jnp.float32)
    inputs = jnp.take(embeds, flat_rows, axis=0).astype(jnp.float32)
    residual = jnp.take(grad_resid, flat_rows, axis=0).astype(jnp.float32)
    scaled = norm_gain.astype(jnp.float32)[None, :] * normal_grad
    squares = lax.optimization_barrier(jnp.sum(inputs * inputs, axis=1))
    inner_sum = lax.optimization_barrier(jnp.sum(scaled * inputs, axis=1))
    inverse = lax.rsqrt(squares / D + NORM_EPS)
    handoff = residual + inverse[:, None] * scaled - inputs * (inverse ** 3 * inner_sum / D)[:, None]
    handoff = handoff.astype(jnp.bfloat16)
    is_live = jnp.arange(IMG_MAX, dtype=jnp.int32)[None, :] < img_count[:, None]
    dest_hot = ((img_dest[:, :, None] == jnp.arange(N_DP, dtype=jnp.int32)[None, None, :]) & is_live[:, :, None]).astype(jnp.int32)
    earlier = jnp.cumsum(dest_hot, axis=1) - dest_hot
    slot_index = lax.optimization_barrier(jnp.sum(earlier * dest_hot, axis=2))
    target = img_dest * ENC_DEV + jnp.arange(N_DP, dtype=jnp.int32)[:, None] * CAP + slot_index
    target = jnp.where(is_live, target, ENC_ROWS).astype(jnp.int32).reshape(-1)
    received = jnp.zeros((ENC_ROWS, D), jnp.bfloat16).at[target].set(handoff, mode='drop')
    model_local = D // N_TENSOR
    hidden_grad = jnp.zeros((ENC_ROWS, MH), jnp.float32)
    for part_index in range(N_TENSOR):
        lower = part_index * model_local
        term = jnp.dot(received[:, lower:lower + model_local], merge_weight[:, lower:lower + model_local].T, preferred_element_type=jnp.float32)
        term = lax.optimization_barrier(term.astype(jnp.bfloat16))
        hidden_grad = hidden_grad + term.astype(jnp.float32)
    return hidden_grad * gelu_slope(merge_pre)
```

```python
import jax
import jax.numpy as jnp
from jax import lax
from jax.sharding import PartitionSpec as P

NORM_EPS = 1e-06


def gelu_slope(pre):
    value = pre.astype(jnp.float32)
    cdf_part = 0.5 * (1.0 + lax.erf(value * 0.7071067811865476))
    pdf_part = jnp.exp(-0.5 * value * value) * 0.3989422804014327
    return cdf_part + value * pdf_part


def transposed_product(left, right):
    return lax.dot_general(
        left, right, (((1,), (1,)), ((), ())), preferred_element_type=jnp.float32
    )


def targets(img_count, img_dest, groups, capacity):
    image_count = img_dest.shape[1]
    is_live = jnp.arange(image_count, dtype=jnp.int32) < img_count[0]
    target_dev = img_dest[0]
    dest_hot = (
        (target_dev[:, None] == jnp.arange(groups, dtype=jnp.int32)[None, :]) & is_live[:, None]
    ).astype(jnp.int32)
    earlier = jnp.cumsum(dest_hot, axis=0) - dest_hot
    slot_index = jnp.sum(earlier * dest_hot, axis=1)
    return jnp.where(is_live, target_dev * capacity + slot_index, -1)


def local(
    grad_query,
    query_weight,
    grad_resid,
    embeds,
    norm_gain,
    img_pos,
    img_count,
    img_dest,
    merge_weight,
    merge_pre,
):
    groups = lax.axis_size("dp")
    parts = lax.axis_size("tensor")
    capacity = merge_pre.shape[0] // groups
    positions = img_pos[0]
    image_count = positions.shape[0]
    rows = image_count // parts
    block = query_weight.shape[0]
    width = block * groups
    picked = lax.all_gather(jnp.take(grad_query, positions, axis=0), "dp", axis=0, tiled=True)
    inputs = jnp.take(embeds, positions, axis=0)
    residual = jnp.take(grad_resid, positions, axis=0)
    inputs = lax.all_to_all(inputs, "tensor", split_axis=0, concat_axis=1, tiled=True)
    residual = lax.all_to_all(residual, "tensor", split_axis=0, concat_axis=1, tiled=True)
    inputs = inputs.astype(jnp.float32)
    gain = lax.all_gather(norm_gain, "tensor", axis=0, tiled=True)
    target = targets(img_count, img_dest, groups, capacity)
    target = lax.all_gather(target, "dp", axis=0)

    partial_value = transposed_product(picked, query_weight).astype(jnp.bfloat16)
    partial_value = partial_value.reshape(groups, parts, rows, block)
    summed = lax.psum_scatter(partial_value, "tensor", scatter_dimension=1, tiled=False)
    normal_grad = lax.all_to_all(summed, "dp", split_axis=0, concat_axis=0, tiled=True)
    normal_grad = normal_grad.transpose(1, 0, 2).reshape(rows, width).astype(jnp.float32)

    scaled = gain[None, :] * normal_grad
    squares = jnp.sum(inputs * inputs, axis=1)
    inner_sum = jnp.sum(scaled * inputs, axis=1)
    inverse = lax.rsqrt(squares / width + NORM_EPS)
    handoff = (
        residual.astype(jnp.float32)
        + inverse[:, None] * scaled
        - inputs * (inverse**3 * inner_sum / width)[:, None]
    )
    handoff = handoff.astype(jnp.bfloat16)
    handoff = lax.all_to_all(handoff, "tensor", split_axis=1, concat_axis=0, tiled=True)
    handoff = lax.all_gather(handoff, "dp", axis=0, tiled=True)

    hidden = transposed_product(handoff, merge_weight).astype(jnp.bfloat16)
    hidden_block = hidden.shape[1]
    hidden = hidden.reshape(groups, image_count, hidden_block)
    placing = jnp.arange(groups * capacity, dtype=jnp.int32)[None, :, None] == target[:, None, :]
    placed = jnp.einsum(
        "spj,sjh->sph", placing.astype(jnp.bfloat16), hidden, preferred_element_type=jnp.float32
    ).astype(jnp.bfloat16)
    placed = placed.reshape(groups, groups, capacity, hidden_block).transpose(1, 0, 2, 3)
    placed = placed.reshape(groups, parts, groups * capacity // parts, hidden_block)
    summed = lax.psum_scatter(placed, "tensor", scatter_dimension=1, tiled=False)
    summed = lax.all_to_all(summed, "dp", split_axis=0, concat_axis=0, tiled=True)
    summed = summed.transpose(1, 0, 2).reshape(groups * capacity // parts, groups * hidden_block)
    hidden_grad = lax.all_to_all(summed, "tensor", split_axis=1, concat_axis=0, tiled=True)
    return hidden_grad.astype(jnp.float32) * gelu_slope(merge_pre)


def solution(mesh):
    in_specs = (
        P("dp", "tensor"),
        P("dp", "tensor"),
        P("dp", "tensor"),
        P("dp", "tensor"),
        P("tensor"),
        P("dp", None),
        P("dp"),
        P("dp", None),
        P("dp", "tensor"),
        P("dp", "tensor"),
    )
    out_specs = P("dp", "tensor")
    return jax.shard_map(local, mesh=mesh, in_specs=in_specs, out_specs=out_specs, check_vma=False)
```

```python
import functools

import jax
import jax.numpy as jnp
from jax import lax
from jax.experimental import pallas as pl
from jax.experimental.pallas import tpu as pltpu
from jax.sharding import PartitionSpec as P

NORM_EPS = 1e-06


def gelu_slope(pre):
    value = pre.astype(jnp.float32)
    cdf_part = 0.5 * (1.0 + lax.erf(value * 0.7071067811865476))
    pdf_part = jnp.exp(-0.5 * value * value) * 0.3989422804014327
    return cdf_part + value * pdf_part


def transposed_product(left, right):
    return lax.dot_general(
        left, right, (((1,), (1,)), ((), ())), preferred_element_type=jnp.float32
    )


def targets(img_count, img_dest, groups, capacity):
    image_count = img_dest.shape[1]
    is_live = jnp.arange(image_count, dtype=jnp.int32) < img_count[0]
    target_dev = img_dest[0]
    dest_hot = (
        (target_dev[:, None] == jnp.arange(groups, dtype=jnp.int32)[None, :]) & is_live[:, None]
    ).astype(jnp.int32)
    earlier = jnp.cumsum(dest_hot, axis=0) - dest_hot
    slot_index = jnp.sum(earlier * dest_hot, axis=1)
    return jnp.where(is_live, target_dev * capacity + slot_index, -1)


def local(
    grad_query,
    query_weight,
    grad_resid,
    embeds,
    norm_gain,
    img_pos,
    img_count,
    img_dest,
    merge_weight,
    merge_pre,
):
    groups = lax.axis_size("dp")
    parts = lax.axis_size("tensor")
    capacity = merge_pre.shape[0] // groups
    positions = img_pos[0]
    image_count = positions.shape[0]
    rows = image_count // parts
    block = query_weight.shape[0]
    width = block * groups
    picked = lax.all_gather(jnp.take(grad_query, positions, axis=0), "dp", axis=0, tiled=True)
    inputs = jnp.take(embeds, positions, axis=0)
    residual = jnp.take(grad_resid, positions, axis=0)
    inputs = lax.all_to_all(inputs, "tensor", split_axis=0, concat_axis=1, tiled=True)
    residual = lax.all_to_all(residual, "tensor", split_axis=0, concat_axis=1, tiled=True)
    inputs = inputs.astype(jnp.float32)
    gain = lax.all_gather(norm_gain, "tensor", axis=0, tiled=True)
    target = targets(img_count, img_dest, groups, capacity)
    target = lax.all_gather(target, "dp", axis=0)

    partial_value = transposed_product(picked, query_weight).astype(jnp.bfloat16)
    partial_value = partial_value.reshape(groups, parts, rows, block)
    summed = lax.psum_scatter(partial_value, "tensor", scatter_dimension=1, tiled=False)
    normal_grad = lax.all_to_all(summed, "dp", split_axis=0, concat_axis=0, tiled=True)
    normal_grad = normal_grad.transpose(1, 0, 2).reshape(rows, width).astype(jnp.float32)

    scaled = gain[None, :] * normal_grad
    squares = jnp.sum(inputs * inputs, axis=1)
    inner_sum = jnp.sum(scaled * inputs, axis=1)
    inverse = lax.rsqrt(squares / width + NORM_EPS)
    handoff = (
        residual.astype(jnp.float32)
        + inverse[:, None] * scaled
        - inputs * (inverse**3 * inner_sum / width)[:, None]
    )
    handoff = handoff.astype(jnp.bfloat16)
    handoff = lax.all_to_all(handoff, "tensor", split_axis=1, concat_axis=0, tiled=True)
    handoff = lax.all_gather(handoff, "dp", axis=0, tiled=True)

    hidden = transposed_product(handoff, merge_weight).astype(jnp.bfloat16)
    hidden_block = hidden.shape[1]
    hidden = hidden.reshape(groups, image_count, hidden_block)
    placing = jnp.arange(groups * capacity, dtype=jnp.int32)[None, :, None] == target[:, None, :]
    placed = jnp.einsum(
        "spj,sjh->sph", placing.astype(jnp.bfloat16), hidden, preferred_element_type=jnp.float32
    ).astype(jnp.bfloat16)
    placed = placed.reshape(groups, groups, capacity, hidden_block).transpose(1, 0, 2, 3)
    placed = placed.reshape(groups, parts, groups * capacity // parts, hidden_block)
    summed = lax.psum_scatter(placed, "tensor", scatter_dimension=1, tiled=False)
    summed = lax.all_to_all(summed, "dp", split_axis=0, concat_axis=0, tiled=True)
    summed = summed.transpose(1, 0, 2).reshape(groups * capacity // parts, groups * hidden_block)
    hidden_grad = lax.all_to_all(summed, "tensor", split_axis=1, concat_axis=0, tiled=True)
    return hidden_grad.astype(jnp.float32) * gelu_slope(merge_pre)


Z = 4
CORES = 2
PARTS = 4
UNIT = 16
UNITS = 3
MESH = pl.DeviceIdType.MESH
BF16 = jnp.bfloat16
F32 = jnp.float32


def stage_order(z, step):
    near = jnp.where(z >= 2, Z - 1 - z, z)
    at = jnp.where((near == 1) & (step < 2), 1 - step, step)
    return jnp.where(z >= 2, Z - 1 - at, at)


def remote(src, dst, send, recv, device):
    return pltpu.make_async_remote_copy(
        src_ref=src, dst_ref=dst, send_sem=send, recv_sem=recv, device_id=device, device_id_type=MESH
    )


def fused_kernel(
    capacity,
    gq, pos, count, dest, gain, wq_hbm, em_hbm, gr_hbm, wm_hbm, mp_hbm,
    out,
    wq, em, gr, wm, mp, slope,
    x, part, part_in, sums, grads,
    x_send, x_in, r_send, r_in, gains, rows_at,
    h_send, h, q, q_in, u, w, f,
    local_sem, x_s, x_r, part_s, part_r, sums_s, grads_r,
    em_s, em_r, gr_s, gr_r, gain_s, gain_r, at_s, at_r,
    hs_s, h_s, h_r, q_s, q_r, u_s, w_r, w_s, f_r,
):
    s = lax.axis_index("dp")
    t = lax.axis_index("tensor")
    z = s // CORES
    c = s % CORES
    groups = Z * CORES
    sib = z * CORES + 1 - c
    sibling = (sib, t)
    tokens = gq.shape[0]
    image_count = pos.shape[1]
    rows = image_count // PARTS
    block = wq.shape[0]
    width = block * groups
    hidden = wm.shape[0]
    middle = (z == 1) | (z == 2)

    loads = [
        pltpu.make_async_copy(src, dst, local_sem.at[i])
        for i, (src, dst) in enumerate(
            ((em_hbm, em), (gr_hbm, gr), (wq_hbm, wq), (mp_hbm, mp), (wm_hbm, wm))
        )
    ]
    for load in loads:
        load.start()

    barrier = pltpu.get_barrier_semaphore()
    for k in range(1, groups):
        pl.semaphore_signal(barrier, inc=1, device_id=((s + k) % groups, t), device_id_type=MESH)
    for k in range(1, PARTS):
        pl.semaphore_signal(barrier, inc=1, device_id=(s, (t + k) % PARTS), device_id_type=MESH)

    hot = (lax.broadcasted_iota(jnp.int32, (tokens, image_count), 0) == pos[...]).astype(F32).astype(BF16)

    def pick(ref):
        return lax.dot_general(
            hot, ref[...], (((0,), (0,)), ((), ())), preferred_element_type=F32
        ).astype(BF16)

    x[pl.ds(s, 1)] = pick(gq)[None]
    pl.semaphore_wait(barrier, groups - 1 + PARTS - 1)

    def to_right(b, d):
        return remote(x.at[b], x.at[b], x_s.at[b, 0], x_r.at[b], (s + CORES, t))

    def to_left(b, d):
        return remote(x.at[b], x.at[b], x_s.at[b, 1], x_r.at[b], (s - CORES, t))

    def to_sibling(b, d):
        return remote(x.at[b], x.at[b], x_s.at[b, 2], x_r.at[b], sibling)

    def h_right(b, d):
        return remote(h.at[b, d], h.at[b, d], h_s.at[b, d, 0], h_r.at[b, d], (s + CORES, t))

    def h_left(b, d):
        return remote(h.at[b, d], h.at[b, d], h_s.at[b, d, 1], h_r.at[b, d], (s - CORES, t))

    def h_sibling(b, d):
        return remote(h.at[b, d], h.at[b, d], h_s.at[b, d, 2], h_r.at[b, d], sibling)

    def spread(act, kinds, zz, d):
        b = zz * CORES + c
        right, left, side = kinds

        @pl.when((zz <= z) & (z < Z - 1))
        def _():
            act(right(b, d))

        @pl.when((zz >= z) & (z > 0))
        def _():
            act(left(b, d))

        act(side(b, d))

    def start(copy):
        copy.start()

    def sent(copy):
        copy.wait_send()

    x_kinds = (to_right, to_left, to_sibling)
    h_kinds = (h_right, h_left, h_sibling)
    spread(start, x_kinds, z, 0)

    def peer(k):
        return (t + k) % PARTS

    gains[pl.ds(t, 1)] = jnp.broadcast_to(gain[...], (1, 8, gain.shape[1]))
    loads[0].wait()
    x_send[...] = pick(em).reshape(x_send.shape)
    loads[1].wait()
    r_send[...] = pick(gr).reshape(r_send.shape)

    def row_copies(k):
        p = peer(k)
        return (
            remote(x_send.at[p], x_in.at[t], em_s.at[k], em_r.at[t], (s, p)),
            remote(r_send.at[p], r_in.at[t], gr_s.at[k], gr_r.at[t], (s, p)),
            remote(gains.at[t], gains.at[t], gain_s.at[k], gain_r.at[t], (s, p)),
        )

    for k in range(1, PARTS):
        for copy in row_copies(k):
            copy.start()
    x_in[pl.ds(t, 1)] = x_send[pl.ds(t, 1)]
    r_in[pl.ds(t, 1)] = r_send[pl.ds(t, 1)]

    lane = lax.broadcasted_iota(jnp.int32, (groups, image_count), 1)
    hot_dest = (dest[...] == lax.broadcasted_iota(jnp.int32, (groups, image_count), 0)) & (lane < count[0])
    hot_dest = hot_dest.astype(F32)
    before = (
        lax.broadcasted_iota(jnp.int32, (image_count, image_count), 0)
        < lax.broadcasted_iota(jnp.int32, (image_count, image_count), 1)
    ).astype(F32)
    earlier = jnp.dot(hot_dest, before, preferred_element_type=F32)
    slot = jnp.sum(earlier * hot_dest, axis=0, keepdims=True).astype(jnp.int32)
    spot = c * capacity + slot
    at = lax.shift_right_logical(spot, 4) * (groups * UNIT) + dest[...] * UNIT + (spot & (UNIT - 1))
    at = jnp.where(lane[:1] < count[0], at, -1)
    rows_at[pl.ds(s, 1)] = jnp.broadcast_to(at, (1, 8, image_count))

    def at_copy(k):
        return remote(rows_at.at[s], rows_at.at[s], at_s.at[k], at_r.at[s], ((s + k) % groups, t))

    for k in range(1, groups):
        at_copy(k).start()

    def part_copy(zz, k):
        p = peer(k)
        return remote(part.at[zz, p], part_in.at[zz, t], part_s.at[zz, k], part_r.at[zz, t], (s, p))

    def sums_copy(zz, cc):
        return remote(
            sums.at[zz, cc], grads.at[s], sums_s.at[zz, cc], grads_r.at[s], (zz * CORES + cc, t)
        )

    def arrived(ref, sem):
        remote(ref, ref, x_s.at[0, 0], sem, sibling).wait_recv()

    def add_parts(zz):
        total = part[zz, t].astype(F32)
        for k in range(1, PARTS):
            p = peer(k)
            arrived(part_in.at[zz, p], part_r.at[zz, p])
            total += part_in[zz, p].astype(F32)
        sums[pl.ds(zz, 1)] = total.astype(BF16)[None]
        for cc in range(CORES):
            own = (zz == z) & (c == cc)

            @pl.when(jnp.logical_not(own))
            def _():
                sums_copy(zz, cc).start()

            @pl.when(own)
            def _():
                grads[pl.ds(s, 1)] = sums[zz, cc][None]

    loads[2].wait()

    def pass_on(zz):
        b = zz * CORES + c
        arrived(x.at[b], x_r.at[b])
        spread(start, x_kinds, zz, 0)

    def first_step(step, carry):
        zz = stage_order(z, step)

        @pl.when((step == 1) | (step == 3) | ((step == 2) & jnp.logical_not(middle)))
        def _():
            pass_on(zz)

        @pl.when((step == 1) & middle)
        def _():
            pass_on(stage_order(z, 2))

        b = zz * CORES + 1 - c
        arrived(x.at[b], x_r.at[b])
        left = x[pl.ds(zz * CORES, CORES)].reshape(CORES * image_count, -1)
        tile = 256
        for n in range(0, block, tile):
            piece = transposed_product(left, wq[n:n + tile]).astype(BF16)
            piece = piece.reshape(CORES, PARTS, rows, tile)
            for p in range(PARTS):
                part[pl.ds(zz, 1), p, :, :, n:n + tile] = piece[:, p][None]
        for k in range(1, PARTS):
            part_copy(zz, k).start()

        @pl.when(step == 0)
        def _():
            loads[3].wait()

            def some_rows(i, carry):
                span = pl.ds(pl.multiple_of(i * UNIT, UNIT), UNIT)
                slope[span] = gelu_slope(mp[span])
                return carry

            lax.fori_loop(0, mp.shape[0] // UNIT, some_rows, 0)

        @pl.when(step > 0)
        def _():
            add_parts(stage_order(z, step - 1))

        return carry

    lax.fori_loop(0, Z, first_step, 0)
    for k in range(1, PARTS):
        p = peer(k)
        arrived(x_in.at[p], em_r.at[p])
        arrived(r_in.at[p], gr_r.at[p])
        arrived(gains.at[p], gain_r.at[p])
    squares = jnp.zeros((rows, 1), F32)
    for p in range(PARTS):
        value = x_in[p].astype(F32)
        squares += jnp.sum(value * value, axis=1, keepdims=True)
    inverse = lax.rsqrt(squares / width + NORM_EPS)
    add_parts(stage_order(z, Z - 1))

    for k in range(1, groups):
        b = (s + k) % groups
        arrived(grads.at[b], grads_r.at[b])

    def scaled_block(b):
        lo = (b % 2) * block
        return gains[b // 2, 0:1, lo:lo + block] * grads[b].astype(F32)

    inner = jnp.zeros((rows, 1), F32)
    for b in range(groups):
        lo = (b % 2) * block
        value = x_in[b // 2, :, lo:lo + block].astype(F32)
        inner += jnp.sum(scaled_block(b) * value, axis=1, keepdims=True)
    back = inverse * inverse * inverse * inner / width
    for b in range(groups):
        lo = (b % 2) * block
        value = x_in[b // 2, :, lo:lo + block].astype(F32)
        residual = r_in[b // 2, :, lo:lo + block].astype(F32)
        result = residual + inverse * scaled_block(b) - value * back
        h_send[b // 2, :, lo:lo + block] = result.astype(BF16)

    def hand_copy(k):
        p = peer(k)
        return remote(h_send.at[p], h.at[s, t], hs_s.at[k], h_r.at[s, t], (s, p))

    for k in range(1, PARTS):
        hand_copy(k).start()
    h[pl.ds(s, 1), pl.ds(t, 1)] = h_send[pl.ds(t, 1)][None]
    for k in range(PARTS):
        d = peer(k)
        if k:
            arrived(h.at[s, d], h_r.at[s, d])
        spread(start, h_kinds, z, d)

    for k in range(1, groups):
        b = (s + k) % groups
        arrived(rows_at.at[b], at_r.at[b])
    loads[4].wait()

    def unit_of(p, zz):
        return (p + zz) % PARTS

    def q_copy(zz, k):
        p = peer(k)
        return remote(
            q.at[zz, unit_of(p, zz)], q_in.at[zz, t], q_s.at[zz, k], q_r.at[zz, t], (s, p)
        )

    def u_copy(zz, r):
        return remote(u.at[zz, r], w.at[s, zz], u_s.at[zz, r], w_r.at[s, zz], (r, t))

    def add_units(zz):
        @pl.when(unit_of(t, zz) < UNITS)
        def _():
            total = q[zz, unit_of(t, zz)].astype(F32)
            for k in range(1, PARTS):
                p = peer(k)
                arrived(q_in.at[zz, p], q_r.at[zz, p])
                total += q_in[zz, p].astype(F32)
            u[pl.ds(zz, 1)] = total.astype(BF16)[None]
            for k in range(1, groups):
                u_copy(zz, (s + k) % groups).start()
            w[pl.ds(s, 1), pl.ds(zz, 1)] = u[zz, s][None, None]

    def h_pass(zz, k):
        b = zz * CORES + c
        d = peer(k)
        arrived(h.at[b, d], h_r.at[b, d])
        spread(start, h_kinds, zz, d)

    def second_step(step, carry):
        zz = stage_order(z, step)
        for k in range(PARTS):
            @pl.when((step == 1) | (step == 3) | ((step == 2) & jnp.logical_not(middle)))
            def _():
                h_pass(zz, k)

            @pl.when((step == 1) & middle)
            def _():
                h_pass(stage_order(z, 2), k)

        b = zz * CORES + 1 - c
        for k in range(PARTS):
            d = peer(k)
            arrived(h.at[b, d], h_r.at[b, d])
        left = h[pl.ds(zz * CORES, CORES)].reshape(CORES * image_count, -1)
        spots = jnp.concatenate([rows_at[zz * CORES, 0:1], rows_at[zz * CORES + 1, 0:1]], axis=1)
        placed_rows = UNITS * groups * UNIT
        place = lax.broadcasted_iota(jnp.int32, (placed_rows, CORES * image_count), 0) == spots
        place = place.astype(F32).astype(BF16)
        lo = 0
        while lo < hidden:
            hi = min(lo + 256, hidden)
            piece = transposed_product(left, wm[lo:hi]).astype(BF16)
            piece = jnp.dot(place, piece, preferred_element_type=F32).astype(BF16)
            q[pl.ds(zz, 1), :, :, :, lo:hi] = piece.reshape(1, UNITS, groups, UNIT, hi - lo)
            lo = hi
        for k in range(1, PARTS):
            @pl.when(unit_of(peer(k), zz) < UNITS)
            def _():
                q_copy(zz, k).start()

        @pl.when(step > 0)
        def _():
            add_units(stage_order(z, step - 1))

        return carry

    lax.fori_loop(0, Z, second_step, 0)
    add_units(stage_order(z, Z - 1))

    def f_copy(b, zz):
        unit = zz * UNITS + unit_of(t, zz)
        return remote(w.at[b, zz], f.at[unit, b % 2], w_s.at[b, zz], f_r.at[unit, b % 2], (s, b // 2))

    def hand_out(i, carry):
        step, k = i // groups, i % groups
        b = (s + k) % groups
        zz = stage_order(b // CORES, step)

        @pl.when(unit_of(t, zz) < UNITS)
        def _():
            @pl.when(b != s)
            def _():
                arrived(w.at[b, zz], w_r.at[b, zz])

            @pl.when(b // 2 != t)
            def _():
                f_copy(b, zz).start()

            @pl.when(b // 2 == t)
            def _():
                unit = zz * UNITS + unit_of(t, zz)
                f[pl.ds(unit, 1), pl.ds(b % 2, 1)] = w[b, zz][None, None]

        return carry

    lax.fori_loop(0, Z * groups, hand_out, 0)

    def finish(unit, carry):
        zz, k = unit // UNITS, unit % UNITS
        span = pl.ds(pl.multiple_of(unit * UNIT, UNIT), UNIT)
        for half in range(2):
            @pl.when((k + PARTS - zz) % PARTS != t)
            def _():
                arrived(f.at[unit, half], f_r.at[unit, half])

            columns = slice(half * hidden, (half + 1) * hidden)
            out[span, columns] = f[unit, half].astype(F32) * slope[span, columns]
        return carry

    lax.fori_loop(0, Z * UNITS, finish, 0)

    for k in range(1, PARTS):
        for copy in row_copies(k):
            sent(copy)
        sent(hand_copy(k))
    for k in range(1, groups):
        sent(at_copy(k))

    def all_sent(zz, carry):
        spread(sent, x_kinds, zz, 0)
        for d in range(PARTS):
            spread(sent, h_kinds, zz, d)
        for k in range(1, PARTS):
            sent(part_copy(zz, k))

            @pl.when(unit_of(peer(k), zz) < UNITS)
            def _():
                sent(q_copy(zz, k))

        for cc in range(CORES):
            @pl.when((zz != z) | (c != cc))
            def _():
                sent(sums_copy(zz, cc))

        @pl.when(unit_of(t, zz) < UNITS)
        def _():
            for k in range(1, groups):
                sent(u_copy(zz, (s + k) % groups))
            for b in range(groups):
                @pl.when(b // 2 != t)
                def _():
                    sent(f_copy(b, zz))

        return carry

    lax.fori_loop(0, Z, all_sent, 0)


def fused(grad_query, query_weight, grad_resid, embeds, norm_gain, img_pos, img_count, img_dest, merge_weight, merge_pre):
    groups = Z * CORES
    capacity = merge_pre.shape[0] // groups
    image_count = img_pos.shape[1]
    rows = image_count // PARTS
    block, columns = query_weight.shape
    hidden = merge_weight.shape[0]
    vmem = pltpu.VMEM
    dma = pltpu.SemaphoreType.DMA
    in_vmem = pl.BlockSpec(memory_space=pltpu.VMEM)
    anywhere = pl.BlockSpec(memory_space=pl.ANY)
    scratch = [
        vmem(query_weight.shape, BF16), vmem(embeds.shape, BF16), vmem(grad_resid.shape, BF16),
        vmem(merge_weight.shape, BF16), vmem(merge_pre.shape, BF16), vmem(merge_pre.shape, F32),
        vmem((groups, image_count, columns), BF16),
        vmem((Z, PARTS, CORES, rows, block), BF16), vmem((Z, PARTS, CORES, rows, block), BF16),
        vmem((Z, CORES, rows, block), BF16), vmem((groups, rows, block), BF16),
        vmem((PARTS, rows, columns), BF16), vmem((PARTS, rows, columns), BF16),
        vmem((PARTS, rows, columns), BF16), vmem((PARTS, rows, columns), BF16),
        vmem((PARTS, 8, columns), F32), vmem((groups, 8, image_count), jnp.int32),
        vmem((PARTS, rows, columns), BF16), vmem((groups, PARTS, rows, columns), BF16),
        vmem((Z, UNITS, groups, UNIT, hidden), BF16), vmem((Z, PARTS, groups, UNIT, hidden), BF16),
        vmem((Z, groups, UNIT, hidden), BF16), vmem((groups, Z, UNIT, hidden), BF16),
        vmem((Z * UNITS, 2, UNIT, hidden), BF16),
        dma((5,)), dma((groups, 3)), dma((groups,)), dma((Z, PARTS)), dma((Z, PARTS)),
        dma((Z, CORES)), dma((groups,)),
        dma((PARTS,)), dma((PARTS,)), dma((PARTS,)), dma((PARTS,)), dma((PARTS,)), dma((PARTS,)),
        dma((groups,)), dma((groups,)),
        dma((PARTS,)), dma((groups, PARTS, 3)), dma((groups, PARTS)), dma((Z, PARTS)), dma((Z, PARTS)),
        dma((Z, groups)), dma((groups, Z)), dma((groups, Z)), dma((Z * UNITS, 2)),
    ]
    return pl.pallas_call(
        functools.partial(fused_kernel, capacity),
        out_shape=jax.ShapeDtypeStruct(merge_pre.shape, F32),
        in_specs=[
            in_vmem, in_vmem, pl.BlockSpec(memory_space=pltpu.SMEM), in_vmem, in_vmem,
            anywhere, anywhere, anywhere, anywhere, anywhere,
        ],
        out_specs=in_vmem,
        scratch_shapes=scratch,
        compiler_params=pltpu.CompilerParams(
            collective_id=0, has_side_effects=True, vmem_limit_bytes=56 * 1024 * 1024
        ),
        cost_estimate=pl.CostEstimate(
            flops=4 * groups * image_count * columns * (block + hidden),
            bytes_accessed=16 * 1024 * 1024,
            transcendentals=merge_pre.size,
        ),
    )(
        grad_query, img_pos, img_count, img_dest, norm_gain.reshape(1, -1),
        query_weight, embeds, grad_resid, merge_weight, merge_pre,
    )


def solution(mesh):
    in_specs = (
        P("dp", "tensor"),
        P("dp", "tensor"),
        P("dp", "tensor"),
        P("dp", "tensor"),
        P("tensor"),
        P("dp", None),
        P("dp"),
        P("dp", None),
        P("dp", "tensor"),
        P("dp", "tensor"),
    )
    out_specs = P("dp", "tensor")
    known = mesh.shape["dp"] == Z * CORES and mesh.shape["tensor"] == PARTS
    body = fused if known else local
    return jax.shard_map(body, mesh=mesh, in_specs=in_specs, out_specs=out_specs, check_vma=False)
```

```python
import functools

import jax
import jax.numpy as jnp
from jax import lax
from jax.experimental import pallas as pl
from jax.experimental.pallas import tpu as pltpu
from jax.sharding import PartitionSpec as P

NORM_EPS = 1e-06


def gelu_slope(pre):
    value = pre.astype(jnp.float32)
    cdf_part = 0.5 * (1.0 + lax.erf(value * 0.7071067811865476))
    pdf_part = jnp.exp(-0.5 * value * value) * 0.3989422804014327
    return cdf_part + value * pdf_part


def transposed_product(left, right):
    return lax.dot_general(
        left, right, (((1,), (1,)), ((), ())), preferred_element_type=jnp.float32
    )


def targets(img_count, img_dest, groups, capacity):
    image_count = img_dest.shape[1]
    is_live = jnp.arange(image_count, dtype=jnp.int32) < img_count[0]
    target_dev = img_dest[0]
    dest_hot = (
        (target_dev[:, None] == jnp.arange(groups, dtype=jnp.int32)[None, :]) & is_live[:, None]
    ).astype(jnp.int32)
    earlier = jnp.cumsum(dest_hot, axis=0) - dest_hot
    slot_index = jnp.sum(earlier * dest_hot, axis=1)
    return jnp.where(is_live, target_dev * capacity + slot_index, -1)


def local(
    grad_query,
    query_weight,
    grad_resid,
    embeds,
    norm_gain,
    img_pos,
    img_count,
    img_dest,
    merge_weight,
    merge_pre,
):
    groups = lax.axis_size("dp")
    parts = lax.axis_size("tensor")
    capacity = merge_pre.shape[0] // groups
    positions = img_pos[0]
    image_count = positions.shape[0]
    rows = image_count // parts
    block = query_weight.shape[0]
    width = block * groups
    picked = lax.all_gather(jnp.take(grad_query, positions, axis=0), "dp", axis=0, tiled=True)
    inputs = jnp.take(embeds, positions, axis=0)
    residual = jnp.take(grad_resid, positions, axis=0)
    inputs = lax.all_to_all(inputs, "tensor", split_axis=0, concat_axis=1, tiled=True)
    residual = lax.all_to_all(residual, "tensor", split_axis=0, concat_axis=1, tiled=True)
    inputs = inputs.astype(jnp.float32)
    gain = lax.all_gather(norm_gain, "tensor", axis=0, tiled=True)
    target = targets(img_count, img_dest, groups, capacity)
    target = lax.all_gather(target, "dp", axis=0)

    partial_value = transposed_product(picked, query_weight).astype(jnp.bfloat16)
    partial_value = partial_value.reshape(groups, parts, rows, block)
    summed = lax.psum_scatter(partial_value, "tensor", scatter_dimension=1, tiled=False)
    normal_grad = lax.all_to_all(summed, "dp", split_axis=0, concat_axis=0, tiled=True)
    normal_grad = normal_grad.transpose(1, 0, 2).reshape(rows, width).astype(jnp.float32)

    scaled = gain[None, :] * normal_grad
    squares = jnp.sum(inputs * inputs, axis=1)
    inner_sum = jnp.sum(scaled * inputs, axis=1)
    inverse = lax.rsqrt(squares / width + NORM_EPS)
    handoff = (
        residual.astype(jnp.float32)
        + inverse[:, None] * scaled
        - inputs * (inverse**3 * inner_sum / width)[:, None]
    )
    handoff = handoff.astype(jnp.bfloat16)
    handoff = lax.all_to_all(handoff, "tensor", split_axis=1, concat_axis=0, tiled=True)
    handoff = lax.all_gather(handoff, "dp", axis=0, tiled=True)

    hidden = transposed_product(handoff, merge_weight).astype(jnp.bfloat16)
    hidden_block = hidden.shape[1]
    hidden = hidden.reshape(groups, image_count, hidden_block)
    placing = jnp.arange(groups * capacity, dtype=jnp.int32)[None, :, None] == target[:, None, :]
    placed = jnp.einsum(
        "spj,sjh->sph", placing.astype(jnp.bfloat16), hidden, preferred_element_type=jnp.float32
    ).astype(jnp.bfloat16)
    placed = placed.reshape(groups, groups, capacity, hidden_block).transpose(1, 0, 2, 3)
    placed = placed.reshape(groups, parts, groups * capacity // parts, hidden_block)
    summed = lax.psum_scatter(placed, "tensor", scatter_dimension=1, tiled=False)
    summed = lax.all_to_all(summed, "dp", split_axis=0, concat_axis=0, tiled=True)
    summed = summed.transpose(1, 0, 2).reshape(groups * capacity // parts, groups * hidden_block)
    hidden_grad = lax.all_to_all(summed, "tensor", split_axis=1, concat_axis=0, tiled=True)
    return hidden_grad.astype(jnp.float32) * gelu_slope(merge_pre)


Z = 4
CORES = 2
PARTS = 4
UNIT = 16
UNITS = 3
MESH = pl.DeviceIdType.MESH
BF16 = jnp.bfloat16
F32 = jnp.float32


def stage_order(z, step):
    near = jnp.where(z >= 2, Z - 1 - z, z)
    at = jnp.where((near == 1) & (step < 2), 1 - step, step)
    return jnp.where(z >= 2, Z - 1 - at, at)


def remote(src, dst, send, recv, device):
    return pltpu.make_async_remote_copy(
        src_ref=src, dst_ref=dst, send_sem=send, recv_sem=recv, device_id=device, device_id_type=MESH
    )


def fused_kernel(
    capacity,
    gq, pos, count, dest, gain, wq_hbm, em_hbm, gr_hbm, wm_hbm, mp_hbm,
    out,
    wq, em, gr, wm, mp, slope,
    x, part, part_in, sums, grads,
    em_rows, gr_rows, ng, stat, rows_at,
    h, q, q_in, u, w, f,
    local_sem, x_s, x_r, part_s, part_r, sums_s, grads_r,
    ng_s, ng_r, stat_s, stat_r, at_s, at_r,
    h_s, h_r, q_s, q_r, u_s, w_r, w_s, f_r,
):
    s = lax.axis_index("dp")
    t = lax.axis_index("tensor")
    z = s // CORES
    c = s % CORES
    groups = Z * CORES
    sib = z * CORES + 1 - c
    sibling = (sib, t)
    tokens = gq.shape[0]
    image_count = pos.shape[1]
    half = image_count // 2
    rows = half // PARTS
    block = wq.shape[0]
    width = block * groups
    hidden = wm.shape[0]
    middle = (z == 1) | (z == 2)

    loads = [
        pltpu.make_async_copy(src, dst, local_sem.at[i])
        for i, (src, dst) in enumerate(
            ((em_hbm, em), (gr_hbm, gr), (wq_hbm, wq), (mp_hbm, mp), (wm_hbm, wm))
        )
    ]
    for load in loads:
        load.start()

    barrier = pltpu.get_barrier_semaphore()
    for k in range(1, groups):
        pl.semaphore_signal(barrier, inc=1, device_id=((s + k) % groups, t), device_id_type=MESH)
    for k in range(1, PARTS):
        pl.semaphore_signal(barrier, inc=1, device_id=(s, (t + k) % PARTS), device_id_type=MESH)

    hot = (lax.broadcasted_iota(jnp.int32, (tokens, image_count), 0) == pos[...]).astype(F32).astype(BF16)

    def pick(ref):
        return lax.dot_general(
            hot, ref[...], (((0,), (0,)), ((), ())), preferred_element_type=F32
        ).astype(BF16)

    x[pl.ds(s, 1)] = pick(gq).reshape(1, 2, half, -1)
    pl.semaphore_wait(barrier, groups - 1 + PARTS - 1)

    def kinds_of(ref, send, recv):
        def make(side, device):
            return lambda b, d: remote(
                ref.at[b, d], ref.at[b, d], send.at[b, d, side], recv.at[b, d], device
            )

        return make(0, (s + CORES, t)), make(1, (s - CORES, t)), make(2, sibling)

    x_kinds = kinds_of(x, x_s, x_r)
    h_kinds = kinds_of(h, h_s, h_r)

    def spread(act, kinds, zz, d):
        b = zz * CORES + c
        right, left, side = kinds

        @pl.when((zz <= z) & (z < Z - 1))
        def _():
            act(right(b, d))

        @pl.when((zz >= z) & (z > 0))
        def _():
            act(left(b, d))

        act(side(b, d))

    def start(copy):
        copy.start()

    def sent(copy):
        copy.wait_send()

    def peer(k):
        return (t + k) % PARTS

    def arrived(ref, sem):
        remote(ref, ref, x_s.at[0, 0, 0], sem, sibling).wait_recv()

    def pass_on(ref, recv, kinds, zz, d):
        b = zz * CORES + c
        arrived(ref.at[b, d], recv.at[b, d])
        spread(start, kinds, zz, d)

    spread(start, x_kinds, z, 0)

    lane = lax.broadcasted_iota(jnp.int32, (groups, image_count), 1)
    hot_dest = (dest[...] == lax.broadcasted_iota(jnp.int32, (groups, image_count), 0)) & (lane < count[0])
    hot_dest = hot_dest.astype(F32)
    before = (
        lax.broadcasted_iota(jnp.int32, (image_count, image_count), 0)
        < lax.broadcasted_iota(jnp.int32, (image_count, image_count), 1)
    ).astype(F32)
    earlier = jnp.dot(hot_dest, before, preferred_element_type=F32)
    slot = jnp.sum(earlier * hot_dest, axis=0, keepdims=True).astype(jnp.int32)
    spot = c * capacity + slot
    at = lax.shift_right_logical(spot, 4) * (groups * UNIT) + dest[...] * UNIT + (spot & (UNIT - 1))
    at = jnp.where(lane[:1] < count[0], at, -1)
    rows_at[pl.ds(s, 1)] = jnp.broadcast_to(at, (1, 8, image_count))

    def at_copy(k):
        return remote(rows_at.at[s], rows_at.at[s], at_s.at[k], at_r.at[s], ((s + k) % groups, t))

    for k in range(1, groups):
        at_copy(k).start()

    def part_copy(d, zz, k):
        p = peer(k)
        return remote(
            part.at[d, zz, p], part_in.at[d, zz, t], part_s.at[d, zz, k], part_r.at[d, zz, t], (s, p)
        )

    def sums_copy(d, zz, cc):
        return remote(
            sums.at[d, zz, cc], grads.at[d, s], sums_s.at[d, zz, cc], grads_r.at[d, s],
            (zz * CORES + cc, t),
        )

    def add_parts(g):
        d = g // Z
        zz = stage_order(z, g % Z)
        total = part[d, zz, t].astype(F32)
        for k in range(1, PARTS):
            p = peer(k)
            arrived(part_in.at[d, zz, p], part_r.at[d, zz, p])
            total += part_in[d, zz, p].astype(F32)
        sums[pl.ds(d, 1), pl.ds(zz, 1)] = total.astype(BF16)[None, None]
        for cc in range(CORES):
            own = (zz == z) & (c == cc)

            @pl.when(jnp.logical_not(own))
            def _():
                sums_copy(d, zz, cc).start()

            @pl.when(own)
            def _():
                grads[pl.ds(d, 1), pl.ds(s, 1)] = sums[d, zz, cc][None, None]

    def grad_copy(d, k):
        p = peer(k)
        return remote(
            grads.at[d, pl.ds(p * 2, 2)], ng.at[d, t], ng_s.at[d, k], ng_r.at[d, t], (s, p)
        )

    def norm_send(d):
        for k in range(1, groups):
            b = (s + k) % groups
            arrived(grads.at[d, b], grads_r.at[d, b])
        for k in range(1, PARTS):
            grad_copy(d, k).start()
        ng[d, pl.ds(t, 1)] = grads[d, pl.ds(t * 2, 2)][None]

    def stat_copy(d, k):
        return remote(stat.at[d, t], stat.at[d, t], stat_s.at[d, k], stat_r.at[d, t], (s, peer(k)))

    def pieces(d, p):
        for e in range(2):
            lo = e * block
            top = d * half + p * rows
            value = em_rows[top:top + rows, lo:lo + block].astype(F32)
            yield lo, top, value, gain[:, lo:lo + block] * ng[d, p, e].astype(F32)

    def norm_stats(d):
        for k in range(1, PARTS):
            p = peer(k)
            arrived(ng.at[d, p], ng_r.at[d, p])
        side = lax.broadcasted_iota(jnp.int32, (rows, 128), 1)
        for p in range(PARTS):
            squares = jnp.zeros((rows, 1), F32)
            inner = jnp.zeros((rows, 1), F32)
            for lo, top, value, scaled in pieces(d, p):
                squares += jnp.sum(value * value, axis=1, keepdims=True)
                inner += jnp.sum(scaled * value, axis=1, keepdims=True)
            both = jnp.where(side < 64, squares, inner)
            stat[d, pl.ds(t, 1), p * rows:(p + 1) * rows] = both[None]
        for k in range(1, PARTS):
            stat_copy(d, k).start()

    def norm_finish(d):
        for k in range(1, PARTS):
            p = peer(k)
            arrived(stat.at[d, p], stat_r.at[d, p])
        for p in range(PARTS):
            total = jnp.zeros((rows, 128), F32)
            for src in range(PARTS):
                total += stat[d, src, p * rows:(p + 1) * rows]
            inverse = lax.rsqrt(total[:, 0:1] / width + NORM_EPS)
            back = inverse * inverse * inverse * total[:, 64:65] / width
            for lo, top, value, scaled in pieces(d, p):
                residual = gr_rows[top:top + rows, lo:lo + block].astype(F32)
                result = residual + inverse * scaled - value * back
                h[pl.ds(s, 1), d, p * rows:(p + 1) * rows, lo:lo + block] = result.astype(BF16)[None]
        spread(start, h_kinds, z, d)

    loads[2].wait()

    def first_step(g, carry):
        d, step = g // Z, g % Z
        zz = stage_order(z, step)
        passes = (step == 1) | (step == 3) | ((step == 2) & jnp.logical_not(middle))
        late = (g == 2 * Z - 1) & jnp.logical_not(middle)

        @pl.when(passes & jnp.logical_not(late))
        def _():
            pass_on(x, x_r, x_kinds, zz, d)

        @pl.when((step == 1) & middle)
        def _():
            pass_on(x, x_r, x_kinds, stage_order(z, 2), d)

        @pl.when(((g == 3) & middle) | ((g == 1) & jnp.logical_not(middle)))
        def _():
            spread(start, x_kinds, z, 1)

        @pl.when(g == 2 * Z - 1)
        def _():
            norm_stats(0)

        @pl.when(late)
        def _():
            pass_on(x, x_r, x_kinds, zz, d)

        b = zz * CORES + 1 - c
        arrived(x.at[b, d], x_r.at[b, d])
        left = x[pl.ds(zz * CORES, CORES), pl.ds(d, 1)].reshape(CORES * half, -1)
        tile = 256
        for n in range(0, block, tile):
            piece = transposed_product(left, wq[n:n + tile]).astype(BF16)
            piece = piece.reshape(CORES, PARTS, rows, tile)
            for p in range(PARTS):
                part[pl.ds(d, 1), pl.ds(zz, 1), p, :, :, n:n + tile] = piece[:, p][None, None]
        for k in range(1, PARTS):
            part_copy(d, zz, k).start()

        @pl.when(g == 0)
        def _():
            loads[0].wait()
            em_rows[...] = pick(em)
            loads[1].wait()
            gr_rows[...] = pick(gr)
            loads[3].wait()

            def some_rows(i, carry):
                span = pl.ds(pl.multiple_of(i * UNIT, UNIT), UNIT)
                slope[span] = gelu_slope(mp[span])
                return carry

            lax.fori_loop(0, mp.shape[0] // UNIT, some_rows, 0)

        @pl.when(g == 2 * Z - 1)
        def _():
            norm_finish(0)

        @pl.when(g > 0)
        def _():
            add_parts(g - 1)

        @pl.when(g == 2 * Z - 2)
        def _():
            norm_send(0)

        return carry

    lax.fori_loop(0, 2 * Z, first_step, 0)
    add_parts(2 * Z - 1)

    pass_on(h, h_r, h_kinds, stage_order(z, 1), 0)

    @pl.when(middle)
    def _():
        pass_on(h, h_r, h_kinds, stage_order(z, 2), 0)

    norm_send(1)
    norm_stats(1)
    norm_finish(1)

    for k in range(1, groups):
        b = (s + k) % groups
        arrived(rows_at.at[b], at_r.at[b])
    loads[4].wait()

    def unit_of(p, zz):
        return (p + zz) % PARTS

    def q_copy(zz, k):
        p = peer(k)
        return remote(
            q.at[zz, unit_of(p, zz)], q_in.at[zz, t], q_s.at[zz, k], q_r.at[zz, t], (s, p)
        )

    def u_copy(zz, r):
        return remote(u.at[zz, r], w.at[s, zz], u_s.at[zz, r], w_r.at[s, zz], (r, t))

    def add_units(zz):
        @pl.when(unit_of(t, zz) < UNITS)
        def _():
            total = q[zz, unit_of(t, zz)].astype(F32)
            for k in range(1, PARTS):
                p = peer(k)
                arrived(q_in.at[zz, p], q_r.at[zz, p])
                total += q_in[zz, p].astype(F32)
            u[pl.ds(zz, 1)] = total.astype(BF16)[None]
            for k in range(1, groups):
                u_copy(zz, (s + k) % groups).start()
            w[pl.ds(s, 1), pl.ds(zz, 1)] = u[zz, s][None, None]

    def second_step(step, carry):
        zz = stage_order(z, step)
        ends = jnp.logical_not(middle)

        @pl.when((step == 1) | ((step > 1) & ends))
        def _():
            @pl.when(step > 1)
            def _():
                pass_on(h, h_r, h_kinds, zz, 0)

            pass_on(h, h_r, h_kinds, zz, 1)

        @pl.when((step == 1) & middle)
        def _():
            pass_on(h, h_r, h_kinds, stage_order(z, 2), 1)

        b = zz * CORES + 1 - c
        for d in range(2):
            arrived(h.at[b, d], h_r.at[b, d])
        left = h[pl.ds(zz * CORES, CORES)].reshape(CORES * image_count, -1)
        spots = jnp.concatenate([rows_at[zz * CORES, 0:1], rows_at[zz * CORES + 1, 0:1]], axis=1)
        placed_rows = UNITS * groups * UNIT
        place = lax.broadcasted_iota(jnp.int32, (placed_rows, CORES * image_count), 0) == spots
        place = place.astype(F32).astype(BF16)
        lo = 0
        while lo < hidden:
            hi = min(lo + 256, hidden)
            piece = transposed_product(left, wm[lo:hi]).astype(BF16)
            piece = jnp.dot(place, piece, preferred_element_type=F32).astype(BF16)
            q[pl.ds(zz, 1), :, :, :, lo:hi] = piece.reshape(1, UNITS, groups, UNIT, hi - lo)
            lo = hi
        for k in range(1, PARTS):
            @pl.when(unit_of(peer(k), zz) < UNITS)
            def _():
                q_copy(zz, k).start()

        @pl.when((step == 2) & middle)
        def _():
            for d in range(2):
                pass_on(h, h_r, h_kinds, stage_order(z, 3), d)

        @pl.when(step > 0)
        def _():
            add_units(stage_order(z, step - 1))

        return carry

    lax.fori_loop(0, Z, second_step, 0)
    add_units(stage_order(z, Z - 1))

    def f_copy(b, zz):
        unit = zz * UNITS + unit_of(t, zz)
        return remote(w.at[b, zz], f.at[unit, b % 2], w_s.at[b, zz], f_r.at[unit, b % 2], (s, b // 2))

    def hand_out(i, carry):
        step, k = i // groups, i % groups
        b = (s + k) % groups
        zz = stage_order(b // CORES, step)

        @pl.when(unit_of(t, zz) < UNITS)
        def _():
            @pl.when(b != s)
            def _():
                arrived(w.at[b, zz], w_r.at[b, zz])

            @pl.when(b // 2 != t)
            def _():
                f_copy(b, zz).start()

            @pl.when(b // 2 == t)
            def _():
                unit = zz * UNITS + unit_of(t, zz)
                f[pl.ds(unit, 1), pl.ds(b % 2, 1)] = w[b, zz][None, None]

        return carry

    lax.fori_loop(0, Z * groups, hand_out, 0)

    def finish(unit, carry):
        zz, k = unit // UNITS, unit % UNITS
        span = pl.ds(pl.multiple_of(unit * UNIT, UNIT), UNIT)
        for half in range(2):
            @pl.when((k + PARTS - zz) % PARTS != t)
            def _():
                arrived(f.at[unit, half], f_r.at[unit, half])

            columns = slice(half * hidden, (half + 1) * hidden)
            out[span, columns] = f[unit, half].astype(F32) * slope[span, columns]
        return carry

    lax.fori_loop(0, Z * UNITS, finish, 0)

    for k in range(1, groups):
        sent(at_copy(k))
    for d in range(2):
        for k in range(1, PARTS):
            sent(grad_copy(d, k))
            sent(stat_copy(d, k))

    def all_sent(zz, carry):
        for d in range(2):
            spread(sent, x_kinds, zz, d)
            spread(sent, h_kinds, zz, d)
            for k in range(1, PARTS):
                sent(part_copy(d, zz, k))
            for cc in range(CORES):
                @pl.when((zz != z) | (c != cc))
                def _():
                    sent(sums_copy(d, zz, cc))

        for k in range(1, PARTS):
            @pl.when(unit_of(peer(k), zz) < UNITS)
            def _():
                sent(q_copy(zz, k))

        @pl.when(unit_of(t, zz) < UNITS)
        def _():
            for k in range(1, groups):
                sent(u_copy(zz, (s + k) % groups))
            for b in range(groups):
                @pl.when(b // 2 != t)
                def _():
                    sent(f_copy(b, zz))

        return carry

    lax.fori_loop(0, Z, all_sent, 0)


def fused(grad_query, query_weight, grad_resid, embeds, norm_gain, img_pos, img_count, img_dest, merge_weight, merge_pre):
    groups = Z * CORES
    capacity = merge_pre.shape[0] // groups
    image_count = img_pos.shape[1]
    half = image_count // 2
    rows = half // PARTS
    block, columns = query_weight.shape
    hidden = merge_weight.shape[0]
    vmem = pltpu.VMEM
    dma = pltpu.SemaphoreType.DMA
    in_vmem = pl.BlockSpec(memory_space=pltpu.VMEM)
    anywhere = pl.BlockSpec(memory_space=pl.ANY)
    scratch = [
        vmem(query_weight.shape, BF16), vmem(embeds.shape, BF16), vmem(grad_resid.shape, BF16),
        vmem(merge_weight.shape, BF16), vmem(merge_pre.shape, BF16), vmem(merge_pre.shape, F32),
        vmem((groups, 2, half, columns), BF16),
        vmem((2, Z, PARTS, CORES, rows, block), BF16), vmem((2, Z, PARTS, CORES, rows, block), BF16),
        vmem((2, Z, CORES, rows, block), BF16), vmem((2, groups, rows, block), BF16),
        vmem((image_count, columns), BF16), vmem((image_count, columns), BF16),
        vmem((2, PARTS, 2, rows, block), BF16), vmem((2, PARTS, half, 128), F32),
        vmem((groups, 8, image_count), jnp.int32),
        vmem((groups, 2, half, columns), BF16),
        vmem((Z, UNITS, groups, UNIT, hidden), BF16), vmem((Z, PARTS, groups, UNIT, hidden), BF16),
        vmem((Z, groups, UNIT, hidden), BF16), vmem((groups, Z, UNIT, hidden), BF16),
        vmem((Z * UNITS, 2, UNIT, hidden), BF16),
        dma((5,)), dma((groups, 2, 3)), dma((groups, 2)), dma((2, Z, PARTS)), dma((2, Z, PARTS)),
        dma((2, Z, CORES)), dma((2, groups)),
        dma((2, PARTS)), dma((2, PARTS)), dma((2, PARTS)), dma((2, PARTS)), dma((groups,)), dma((groups,)),
        dma((groups, 2, 3)), dma((groups, 2)), dma((Z, PARTS)), dma((Z, PARTS)),
        dma((Z, groups)), dma((groups, Z)), dma((groups, Z)), dma((Z * UNITS, 2)),
    ]
    return pl.pallas_call(
        functools.partial(fused_kernel, capacity),
        out_shape=jax.ShapeDtypeStruct(merge_pre.shape, F32),
        in_specs=[
            in_vmem, in_vmem, pl.BlockSpec(memory_space=pltpu.SMEM), in_vmem, in_vmem,
            anywhere, anywhere, anywhere, anywhere, anywhere,
        ],
        out_specs=in_vmem,
        scratch_shapes=scratch,
        compiler_params=pltpu.CompilerParams(
            collective_id=0, has_side_effects=True, vmem_limit_bytes=56 * 1024 * 1024
        ),
        cost_estimate=pl.CostEstimate(
            flops=4 * groups * image_count * columns * (block + hidden),
            bytes_accessed=16 * 1024 * 1024,
            transcendentals=merge_pre.size,
        ),
    )(
        grad_query, img_pos, img_count, img_dest, norm_gain.reshape(1, -1),
        query_weight, embeds, grad_resid, merge_weight, merge_pre,
    )


def solution(mesh):
    in_specs = (
        P("dp", "tensor"),
        P("dp", "tensor"),
        P("dp", "tensor"),
        P("dp", "tensor"),
        P("tensor"),
        P("dp", None),
        P("dp"),
        P("dp", None),
        P("dp", "tensor"),
        P("dp", "tensor"),
    )
    out_specs = P("dp", "tensor")
    known = mesh.shape["dp"] == Z * CORES and mesh.shape["tensor"] == PARTS
    body = fused if known else local
    return jax.shard_map(body, mesh=mesh, in_specs=in_specs, out_specs=out_specs, check_vma=False)
```

```python
import functools

import jax
import jax.numpy as jnp
from jax import lax
from jax.experimental import pallas as pl
from jax.experimental.pallas import tpu as pltpu
from jax.sharding import PartitionSpec as P

NORM_EPS = 1e-06


def gelu_slope(pre):
    value = pre.astype(jnp.float32)
    cdf_part = 0.5 * (1.0 + lax.erf(value * 0.7071067811865476))
    pdf_part = jnp.exp(-0.5 * value * value) * 0.3989422804014327
    return cdf_part + value * pdf_part


def transposed_product(left, right):
    return lax.dot_general(
        left, right, (((1,), (1,)), ((), ())), preferred_element_type=jnp.float32
    )


def targets(img_count, img_dest, groups, capacity):
    image_count = img_dest.shape[1]
    is_live = jnp.arange(image_count, dtype=jnp.int32) < img_count[0]
    target_dev = img_dest[0]
    dest_hot = (
        (target_dev[:, None] == jnp.arange(groups, dtype=jnp.int32)[None, :]) & is_live[:, None]
    ).astype(jnp.int32)
    earlier = jnp.cumsum(dest_hot, axis=0) - dest_hot
    slot_index = jnp.sum(earlier * dest_hot, axis=1)
    return jnp.where(is_live, target_dev * capacity + slot_index, -1)


def local(
    grad_query,
    query_weight,
    grad_resid,
    embeds,
    norm_gain,
    img_pos,
    img_count,
    img_dest,
    merge_weight,
    merge_pre,
):
    groups = lax.axis_size("dp")
    parts = lax.axis_size("tensor")
    capacity = merge_pre.shape[0] // groups
    positions = img_pos[0]
    image_count = positions.shape[0]
    rows = image_count // parts
    block = query_weight.shape[0]
    width = block * groups
    picked = lax.all_gather(jnp.take(grad_query, positions, axis=0), "dp", axis=0, tiled=True)
    inputs = jnp.take(embeds, positions, axis=0)
    residual = jnp.take(grad_resid, positions, axis=0)
    inputs = lax.all_to_all(inputs, "tensor", split_axis=0, concat_axis=1, tiled=True)
    residual = lax.all_to_all(residual, "tensor", split_axis=0, concat_axis=1, tiled=True)
    inputs = inputs.astype(jnp.float32)
    gain = lax.all_gather(norm_gain, "tensor", axis=0, tiled=True)
    target = targets(img_count, img_dest, groups, capacity)
    target = lax.all_gather(target, "dp", axis=0)

    partial_value = transposed_product(picked, query_weight).astype(jnp.bfloat16)
    partial_value = partial_value.reshape(groups, parts, rows, block)
    summed = lax.psum_scatter(partial_value, "tensor", scatter_dimension=1, tiled=False)
    normal_grad = lax.all_to_all(summed, "dp", split_axis=0, concat_axis=0, tiled=True)
    normal_grad = normal_grad.transpose(1, 0, 2).reshape(rows, width).astype(jnp.float32)

    scaled = gain[None, :] * normal_grad
    squares = jnp.sum(inputs * inputs, axis=1)
    inner_sum = jnp.sum(scaled * inputs, axis=1)
    inverse = lax.rsqrt(squares / width + NORM_EPS)
    handoff = (
        residual.astype(jnp.float32)
        + inverse[:, None] * scaled
        - inputs * (inverse**3 * inner_sum / width)[:, None]
    )
    handoff = handoff.astype(jnp.bfloat16)
    handoff = lax.all_to_all(handoff, "tensor", split_axis=1, concat_axis=0, tiled=True)
    handoff = lax.all_gather(handoff, "dp", axis=0, tiled=True)

    hidden = transposed_product(handoff, merge_weight).astype(jnp.bfloat16)
    hidden_block = hidden.shape[1]
    hidden = hidden.reshape(groups, image_count, hidden_block)
    placing = jnp.arange(groups * capacity, dtype=jnp.int32)[None, :, None] == target[:, None, :]
    placed = jnp.einsum(
        "spj,sjh->sph", placing.astype(jnp.bfloat16), hidden, preferred_element_type=jnp.float32
    ).astype(jnp.bfloat16)
    placed = placed.reshape(groups, groups, capacity, hidden_block).transpose(1, 0, 2, 3)
    placed = placed.reshape(groups, parts, groups * capacity // parts, hidden_block)
    summed = lax.psum_scatter(placed, "tensor", scatter_dimension=1, tiled=False)
    summed = lax.all_to_all(summed, "dp", split_axis=0, concat_axis=0, tiled=True)
    summed = summed.transpose(1, 0, 2).reshape(groups * capacity // parts, groups * hidden_block)
    hidden_grad = lax.all_to_all(summed, "tensor", split_axis=1, concat_axis=0, tiled=True)
    return hidden_grad.astype(jnp.float32) * gelu_slope(merge_pre)


Z = 4
CORES = 2
PARTS = 4
UNIT = 16
TILE = 128
MESH = pl.DeviceIdType.MESH
BF16 = jnp.bfloat16
F32 = jnp.float32


def stage_order(z, step):
    near = jnp.where(z >= 2, Z - 1 - z, z)
    at = jnp.where((near == 1) & (step < 2), 1 - step, step)
    return jnp.where(z >= 2, Z - 1 - at, at)


def remote(src, dst, send, recv, device):
    return pltpu.make_async_remote_copy(
        src_ref=src, dst_ref=dst, send_sem=send, recv_sem=recv, device_id=device, device_id_type=MESH
    )


def fused_kernel(
    capacity,
    gq, pos, count, dest, gain, wq_hbm, em_hbm, gr_hbm, wm_hbm, mp_hbm,
    out,
    wq, em, gr, wm, mp, slope,
    x, part, part_in, sums, grads,
    em_rows, gr_rows, ng, stat, rows_at,
    h, q, q_in, u, w, f,
    local_sem, x_s, x_r, part_s, part_r, sums_s, grads_r,
    ng_s, ng_r, stat_s, stat_r, at_s, at_r,
    h_s, h_r, q_s, q_r, u_s, w_r, w_s, f_r,
):
    s = lax.axis_index("dp")
    t = lax.axis_index("tensor")
    z = s // CORES
    c = s % CORES
    groups = Z * CORES
    sib = z * CORES + 1 - c
    sibling = (sib, t)
    tokens = gq.shape[0]
    image_count = pos.shape[1]
    half = image_count // 2
    rows = half // PARTS
    block = wq.shape[0]
    width = block * groups
    hidden = wm.shape[0]
    tiles = hidden // TILE
    pair_rows = CORES * capacity
    middle = (z == 1) | (z == 2)

    loads = [
        pltpu.make_async_copy(src, dst, local_sem.at[i])
        for i, (src, dst) in enumerate(
            ((em_hbm, em), (gr_hbm, gr), (wq_hbm, wq), (mp_hbm, mp), (wm_hbm, wm))
        )
    ]
    for load in loads:
        load.start()

    barrier = pltpu.get_barrier_semaphore()
    for k in range(1, groups):
        pl.semaphore_signal(barrier, inc=1, device_id=((s + k) % groups, t), device_id_type=MESH)
    for k in range(1, PARTS):
        pl.semaphore_signal(barrier, inc=1, device_id=(s, (t + k) % PARTS), device_id_type=MESH)

    hot = (lax.broadcasted_iota(jnp.int32, (tokens, image_count), 0) == pos[...]).astype(F32).astype(BF16)

    def pick(ref):
        return lax.dot_general(
            hot, ref[...], (((0,), (0,)), ((), ())), preferred_element_type=F32
        ).astype(BF16)

    x[pl.ds(s, 1)] = pick(gq).reshape(1, 2, half, -1)
    pl.semaphore_wait(barrier, groups - 1 + PARTS - 1)

    def kinds_of(ref, send, recv):
        def make(side, device):
            return lambda b, d: remote(
                ref.at[b, d], ref.at[b, d], send.at[b, d, side], recv.at[b, d], device
            )

        return make(0, (s + CORES, t)), make(1, (s - CORES, t)), make(2, sibling)

    x_kinds = kinds_of(x, x_s, x_r)
    h_kinds = kinds_of(h, h_s, h_r)

    def spread(act, kinds, zz, d):
        b = zz * CORES + c
        right, left, side = kinds

        @pl.when((zz <= z) & (z < Z - 1))
        def _():
            act(right(b, d))

        @pl.when((zz >= z) & (z > 0))
        def _():
            act(left(b, d))

        act(side(b, d))

    def start(copy):
        copy.start()

    def sent(copy):
        copy.wait_send()

    def peer(k):
        return (t + k) % PARTS

    def arrived(ref, sem):
        remote(ref, ref, x_s.at[0, 0, 0], sem, sibling).wait_recv()

    def pass_on(ref, recv, kinds, zz, d):
        b = zz * CORES + c
        arrived(ref.at[b, d], recv.at[b, d])
        spread(start, kinds, zz, d)

    spread(start, x_kinds, z, 0)

    lane = lax.broadcasted_iota(jnp.int32, (groups, image_count), 1)
    hot_dest = (dest[...] == lax.broadcasted_iota(jnp.int32, (groups, image_count), 0)) & (lane < count[0])
    hot_dest = hot_dest.astype(F32)
    before = (
        lax.broadcasted_iota(jnp.int32, (image_count, image_count), 0)
        < lax.broadcasted_iota(jnp.int32, (image_count, image_count), 1)
    ).astype(F32)
    earlier = jnp.dot(hot_dest, before, preferred_element_type=F32)
    slot = jnp.sum(earlier * hot_dest, axis=0, keepdims=True).astype(jnp.int32)
    spot = c * capacity + slot
    at = jnp.where(lane[:1] < count[0], dest[...] * pair_rows + spot, -1)
    rows_at[pl.ds(s, 1)] = jnp.broadcast_to(at, (1, 8, image_count))

    def at_copy(k):
        return remote(rows_at.at[s], rows_at.at[s], at_s.at[k], at_r.at[s], ((s + k) % groups, t))

    for k in range(1, groups):
        at_copy(k).start()

    def part_copy(d, zz, k):
        p = peer(k)
        return remote(
            part.at[d, zz, p], part_in.at[d, zz, t], part_s.at[d, zz, k], part_r.at[d, zz, t], (s, p)
        )

    def sums_copy(d, zz, cc):
        return remote(
            sums.at[d, zz, cc], grads.at[d, s], sums_s.at[d, zz, cc], grads_r.at[d, s],
            (zz * CORES + cc, t),
        )

    def add_parts(g):
        d = g // Z
        zz = stage_order(z, g % Z)
        total = part[d, zz, t].astype(F32)
        for k in range(1, PARTS):
            p = peer(k)
            arrived(part_in.at[d, zz, p], part_r.at[d, zz, p])
            total += part_in[d, zz, p].astype(F32)
        sums[pl.ds(d, 1), pl.ds(zz, 1)] = total.astype(BF16)[None, None]
        for cc in range(CORES):
            own = (zz == z) & (c == cc)

            @pl.when(jnp.logical_not(own))
            def _():
                sums_copy(d, zz, cc).start()

            @pl.when(own)
            def _():
                grads[pl.ds(d, 1), pl.ds(s, 1)] = sums[d, zz, cc][None, None]

    def grad_copy(d, k):
        p = peer(k)
        return remote(
            grads.at[d, pl.ds(p * 2, 2)], ng.at[d, t], ng_s.at[d, k], ng_r.at[d, t], (s, p)
        )

    def norm_send(d):
        for k in range(1, groups):
            b = (s + k) % groups
            arrived(grads.at[d, b], grads_r.at[d, b])
        for k in range(1, PARTS):
            grad_copy(d, k).start()
        ng[d, pl.ds(t, 1)] = grads[d, pl.ds(t * 2, 2)][None]

    def stat_copy(d, k):
        return remote(stat.at[d, t], stat.at[d, t], stat_s.at[d, k], stat_r.at[d, t], (s, peer(k)))

    def pieces(d, p):
        for e in range(2):
            lo = e * block
            top = d * half + p * rows
            value = em_rows[top:top + rows, lo:lo + block].astype(F32)
            yield lo, top, value, gain[:, lo:lo + block] * ng[d, p, e].astype(F32)

    def norm_stats(d):
        for k in range(1, PARTS):
            p = peer(k)
            arrived(ng.at[d, p], ng_r.at[d, p])
        side = lax.broadcasted_iota(jnp.int32, (rows, 128), 1)
        for p in range(PARTS):
            squares = jnp.zeros((rows, 1), F32)
            inner = jnp.zeros((rows, 1), F32)
            for lo, top, value, scaled in pieces(d, p):
                squares += jnp.sum(value * value, axis=1, keepdims=True)
                inner += jnp.sum(scaled * value, axis=1, keepdims=True)
            both = jnp.where(side < 64, squares, inner)
            stat[d, pl.ds(t, 1), p * rows:(p + 1) * rows] = both[None]
        for k in range(1, PARTS):
            stat_copy(d, k).start()

    def norm_finish(d):
        for k in range(1, PARTS):
            p = peer(k)
            arrived(stat.at[d, p], stat_r.at[d, p])
        for p in range(PARTS):
            total = jnp.zeros((rows, 128), F32)
            for src in range(PARTS):
                total += stat[d, src, p * rows:(p + 1) * rows]
            inverse = lax.rsqrt(total[:, 0:1] / width + NORM_EPS)
            back = inverse * inverse * inverse * total[:, 64:65] / width
            for lo, top, value, scaled in pieces(d, p):
                residual = gr_rows[top:top + rows, lo:lo + block].astype(F32)
                result = residual + inverse * scaled - value * back
                h[pl.ds(s, 1), d, p * rows:(p + 1) * rows, lo:lo + block] = result.astype(BF16)[None]
        spread(start, h_kinds, z, d)

    loads[2].wait()

    def first_step(g, carry):
        d, step = g // Z, g % Z
        zz = stage_order(z, step)
        passes = (step == 1) | (step == 3) | ((step == 2) & jnp.logical_not(middle))
        late = (g == 2 * Z - 1) & jnp.logical_not(middle)

        @pl.when(passes & jnp.logical_not(late))
        def _():
            pass_on(x, x_r, x_kinds, zz, d)

        @pl.when((step == 1) & middle)
        def _():
            pass_on(x, x_r, x_kinds, stage_order(z, 2), d)

        @pl.when(((g == 3) & middle) | ((g == 1) & jnp.logical_not(middle)))
        def _():
            spread(start, x_kinds, z, 1)

        @pl.when(g == 2 * Z - 1)
        def _():
            norm_stats(0)

        @pl.when(late)
        def _():
            pass_on(x, x_r, x_kinds, zz, d)

        b = zz * CORES + 1 - c
        arrived(x.at[b, d], x_r.at[b, d])
        left = x[pl.ds(zz * CORES, CORES), pl.ds(d, 1)].reshape(CORES * half, -1)
        tile = 256
        for n in range(0, block, tile):
            piece = transposed_product(left, wq[n:n + tile]).astype(BF16)
            piece = piece.reshape(CORES, PARTS, rows, tile)
            for p in range(PARTS):
                part[pl.ds(d, 1), pl.ds(zz, 1), p, :, :, n:n + tile] = piece[:, p][None, None]
        for k in range(1, PARTS):
            part_copy(d, zz, k).start()

        @pl.when(g == 0)
        def _():
            loads[0].wait()
            em_rows[...] = pick(em)
            loads[1].wait()
            gr_rows[...] = pick(gr)
            loads[3].wait()

            def some_rows(i, carry):
                span = pl.ds(pl.multiple_of(i * UNIT, UNIT), UNIT)
                slope[span] = gelu_slope(mp[span])
                return carry

            lax.fori_loop(0, mp.shape[0] // UNIT, some_rows, 0)

        @pl.when(g == 2 * Z - 1)
        def _():
            norm_finish(0)

        @pl.when(g > 0)
        def _():
            add_parts(g - 1)

        @pl.when(g == 2 * Z - 2)
        def _():
            norm_send(0)

        return carry

    lax.fori_loop(0, 2 * Z, first_step, 0)
    add_parts(2 * Z - 1)

    pass_on(h, h_r, h_kinds, stage_order(z, 1), 0)

    @pl.when(middle)
    def _():
        pass_on(h, h_r, h_kinds, stage_order(z, 2), 0)

    norm_send(1)
    norm_stats(1)
    norm_finish(1)

    for k in range(1, groups):
        b = (s + k) % groups
        arrived(rows_at.at[b], at_r.at[b])
    loads[4].wait()

    def first_tile(zz):
        return (t + PARTS - zz) % PARTS

    def held(zz, e):
        return (first_tile(zz) == 0) | (e == 0)

    def tile_of(zz, e):
        return first_tile(zz) if e == 0 else PARTS

    def q_copy(zz, d, j):
        e = j // PARTS
        return remote(
            q.at[zz, d, j], q_in.at[zz, d, e, t], q_s.at[zz, d, j], q_r.at[zz, d, e, t],
            (s, (j + zz) % PARTS),
        )

    def u_copy(zz, e, r):
        return remote(u.at[zz, e, r], w.at[s, zz, e], u_s.at[zz, e, r], w_r.at[s, zz, e], (r, t))

    def add_tiles(zz):
        places = []
        for d in range(2):
            lo = d * half
            spots = jnp.concatenate(
                [rows_at[zz * CORES + cc, 0:1, lo:lo + half] for cc in range(CORES)], axis=1
            )
            hot_rows = lax.broadcasted_iota(jnp.int32, (groups * pair_rows, CORES * half), 0) == spots
            places.append(hot_rows.astype(F32).astype(BF16))
        for e in range(2):
            @pl.when(held(zz, e))
            def _():
                placed = jnp.zeros((groups * pair_rows, TILE), F32)
                for d in range(2):
                    total = q[zz, d, tile_of(zz, e)].astype(F32)
                    for k in range(1, PARTS):
                        p = peer(k)
                        arrived(q_in.at[zz, d, e, p], q_r.at[zz, d, e, p])
                        total += q_in[zz, d, e, p].astype(F32)
                    placed += jnp.dot(places[d], total.astype(BF16), preferred_element_type=F32)
                placed = placed.astype(BF16).reshape(1, 1, groups, pair_rows, TILE)
                u[pl.ds(zz, 1), e:e + 1] = placed
                for k in range(1, groups):
                    u_copy(zz, e, (s + k) % groups).start()
                w[pl.ds(s, 1), pl.ds(zz, 1), e] = u[zz, e, s][None, None]

    def second_step(i, carry):
        step, d = i // 2, i % 2
        zz = stage_order(z, step)
        ends = jnp.logical_not(middle)

        @pl.when((i == 3) | ((i > 3) & ends))
        def _():
            pass_on(h, h_r, h_kinds, zz, d)

        @pl.when((i == 3) & middle)
        def _():
            pass_on(h, h_r, h_kinds, stage_order(z, 2), 1)

        b = zz * CORES + 1 - c
        arrived(h.at[b, d], h_r.at[b, d])
        left = h[pl.ds(zz * CORES, CORES), pl.ds(d, 1)].reshape(CORES * half, -1)
        for j in range(0, tiles, 2):
            hi = min(j + 2, tiles)
            piece = transposed_product(left, wm[j * TILE:hi * TILE]).astype(BF16)
            for jj in range(j, hi):
                q[pl.ds(zz, 1), pl.ds(d, 1), jj] = piece[:, (jj - j) * TILE:(jj - j + 1) * TILE][None, None]
        for j in range(tiles):
            @pl.when((j + zz) % PARTS != t)
            def _():
                q_copy(zz, d, j).start()

        @pl.when(((i == 3) | (i == 5)) & middle)
        def _():
            pass_on(h, h_r, h_kinds, stage_order(z, 3), i // 5)

        @pl.when((i > 1) & (d == 0))
        def _():
            add_tiles(stage_order(z, step - 1))

        return carry

    lax.fori_loop(0, 2 * Z, second_step, 0)
    add_tiles(stage_order(z, Z - 1))

    def f_copy(b, zz, e):
        j = tile_of(zz, e)
        return remote(
            w.at[b, zz, e], f.at[zz, b % 2, j], w_s.at[b, zz, e], f_r.at[zz, b % 2, j], (s, b // 2)
        )

    def hand_out(i, carry):
        step, k = i // groups, i % groups
        b = (s + k) % groups
        zz = stage_order(b // CORES, step)
        for e in range(2):
            @pl.when(held(zz, e))
            def _():
                @pl.when(b != s)
                def _():
                    arrived(w.at[b, zz, e], w_r.at[b, zz, e])

                @pl.when(b // 2 != t)
                def _():
                    f_copy(b, zz, e).start()

                @pl.when(b // 2 == t)
                def _():
                    f[pl.ds(zz, 1), pl.ds(b % 2, 1), pl.ds(tile_of(zz, e), 1)] = w[b, zz, e][None, None, None]

        return carry

    lax.fori_loop(0, Z * groups, hand_out, 0)

    def finish(zz, carry):
        span = pl.ds(pl.multiple_of(zz * pair_rows, pair_rows), pair_rows)
        for side in range(2):
            for j in range(tiles):
                @pl.when((j + zz) % PARTS != t)
                def _():
                    arrived(f.at[zz, side, j], f_r.at[zz, side, j])

                lo = side * hidden + j * TILE
                out[span, lo:lo + TILE] = f[zz, side, j].astype(F32) * slope[span, lo:lo + TILE]
        return carry

    lax.fori_loop(0, Z, finish, 0)

    for k in range(1, groups):
        sent(at_copy(k))
    for d in range(2):
        for k in range(1, PARTS):
            sent(grad_copy(d, k))
            sent(stat_copy(d, k))

    def all_sent(zz, carry):
        for d in range(2):
            spread(sent, x_kinds, zz, d)
            spread(sent, h_kinds, zz, d)
            for k in range(1, PARTS):
                sent(part_copy(d, zz, k))
            for cc in range(CORES):
                @pl.when((zz != z) | (c != cc))
                def _():
                    sent(sums_copy(d, zz, cc))

        for j in range(tiles):
            @pl.when((j + zz) % PARTS != t)
            def _():
                for d in range(2):
                    sent(q_copy(zz, d, j))

        for e in range(2):
            @pl.when(held(zz, e))
            def _():
                for k in range(1, groups):
                    sent(u_copy(zz, e, (s + k) % groups))
                for b in range(groups):
                    @pl.when(b // 2 != t)
                    def _():
                        sent(f_copy(b, zz, e))

        return carry

    lax.fori_loop(0, Z, all_sent, 0)


def fused(grad_query, query_weight, grad_resid, embeds, norm_gain, img_pos, img_count, img_dest, merge_weight, merge_pre):
    groups = Z * CORES
    capacity = merge_pre.shape[0] // groups
    image_count = img_pos.shape[1]
    half = image_count // 2
    rows = half // PARTS
    block, columns = query_weight.shape
    tiles = merge_weight.shape[0] // TILE
    pair_rows = CORES * capacity
    vmem = pltpu.VMEM
    dma = pltpu.SemaphoreType.DMA
    in_vmem = pl.BlockSpec(memory_space=pltpu.VMEM)
    anywhere = pl.BlockSpec(memory_space=pl.ANY)
    scratch = [
        vmem(query_weight.shape, BF16), vmem(embeds.shape, BF16), vmem(grad_resid.shape, BF16),
        vmem(merge_weight.shape, BF16), vmem(merge_pre.shape, BF16), vmem(merge_pre.shape, F32),
        vmem((groups, 2, half, columns), BF16),
        vmem((2, Z, PARTS, CORES, rows, block), BF16), vmem((2, Z, PARTS, CORES, rows, block), BF16),
        vmem((2, Z, CORES, rows, block), BF16), vmem((2, groups, rows, block), BF16),
        vmem((image_count, columns), BF16), vmem((image_count, columns), BF16),
        vmem((2, PARTS, 2, rows, block), BF16), vmem((2, PARTS, half, 128), F32),
        vmem((groups, 8, image_count), jnp.int32),
        vmem((groups, 2, half, columns), BF16),
        vmem((Z, 2, tiles, CORES * half, TILE), BF16), vmem((Z, 2, 2, PARTS, CORES * half, TILE), BF16),
        vmem((Z, 2, groups, pair_rows, TILE), BF16), vmem((groups, Z, 2, pair_rows, TILE), BF16),
        vmem((Z, 2, tiles, pair_rows, TILE), BF16),
        dma((5,)), dma((groups, 2, 3)), dma((groups, 2)), dma((2, Z, PARTS)), dma((2, Z, PARTS)),
        dma((2, Z, CORES)), dma((2, groups)),
        dma((2, PARTS)), dma((2, PARTS)), dma((2, PARTS)), dma((2, PARTS)), dma((groups,)), dma((groups,)),
        dma((groups, 2, 3)), dma((groups, 2)), dma((Z, 2, tiles)), dma((Z, 2, 2, PARTS)),
        dma((Z, 2, groups)), dma((groups, Z, 2)), dma((groups, Z, 2)), dma((Z, 2, tiles)),
    ]
    return pl.pallas_call(
        functools.partial(fused_kernel, capacity),
        out_shape=jax.ShapeDtypeStruct(merge_pre.shape, F32),
        in_specs=[
            in_vmem, in_vmem, pl.BlockSpec(memory_space=pltpu.SMEM), in_vmem, in_vmem,
            anywhere, anywhere, anywhere, anywhere, anywhere,
        ],
        out_specs=in_vmem,
        scratch_shapes=scratch,
        compiler_params=pltpu.CompilerParams(
            collective_id=0, has_side_effects=True, vmem_limit_bytes=56 * 1024 * 1024
        ),
        cost_estimate=pl.CostEstimate(
            flops=4 * groups * image_count * columns * (block + merge_weight.shape[0]),
            bytes_accessed=16 * 1024 * 1024,
            transcendentals=merge_pre.size,
        ),
    )(
        grad_query, img_pos, img_count, img_dest, norm_gain.reshape(1, -1),
        query_weight, embeds, grad_resid, merge_weight, merge_pre,
    )


def solution(mesh):
    in_specs = (
        P("dp", "tensor"),
        P("dp", "tensor"),
        P("dp", "tensor"),
        P("dp", "tensor"),
        P("tensor"),
        P("dp", None),
        P("dp"),
        P("dp", None),
        P("dp", "tensor"),
        P("dp", "tensor"),
    )
    out_specs = P("dp", "tensor")
    known = mesh.shape["dp"] == Z * CORES and mesh.shape["tensor"] == PARTS
    body = fused if known else local
    return jax.shard_map(body, mesh=mesh, in_specs=in_specs, out_specs=out_specs, check_vma=False)
```

```python
import functools

import jax
import jax.numpy as jnp
from jax import lax
from jax.experimental import pallas as pl
from jax.experimental.pallas import tpu as pltpu
from jax.sharding import PartitionSpec as P

NORM_EPS = 1e-06


def gelu_slope(pre):
    value = pre.astype(jnp.float32)
    cdf_part = 0.5 * (1.0 + lax.erf(value * 0.7071067811865476))
    pdf_part = jnp.exp(-0.5 * value * value) * 0.3989422804014327
    return cdf_part + value * pdf_part


def transposed_product(left, right):
    return lax.dot_general(
        left, right, (((1,), (1,)), ((), ())), preferred_element_type=jnp.float32
    )


def targets(img_count, img_dest, groups, capacity):
    image_count = img_dest.shape[1]
    is_live = jnp.arange(image_count, dtype=jnp.int32) < img_count[0]
    target_dev = img_dest[0]
    dest_hot = (
        (target_dev[:, None] == jnp.arange(groups, dtype=jnp.int32)[None, :]) & is_live[:, None]
    ).astype(jnp.int32)
    earlier = jnp.cumsum(dest_hot, axis=0) - dest_hot
    slot_index = jnp.sum(earlier * dest_hot, axis=1)
    return jnp.where(is_live, target_dev * capacity + slot_index, -1)


def local(
    grad_query,
    query_weight,
    grad_resid,
    embeds,
    norm_gain,
    img_pos,
    img_count,
    img_dest,
    merge_weight,
    merge_pre,
):
    groups = lax.axis_size("dp")
    parts = lax.axis_size("tensor")
    capacity = merge_pre.shape[0] // groups
    positions = img_pos[0]
    image_count = positions.shape[0]
    rows = image_count // parts
    block = query_weight.shape[0]
    width = block * groups
    picked = lax.all_gather(jnp.take(grad_query, positions, axis=0), "dp", axis=0, tiled=True)
    inputs = jnp.take(embeds, positions, axis=0)
    residual = jnp.take(grad_resid, positions, axis=0)
    inputs = lax.all_to_all(inputs, "tensor", split_axis=0, concat_axis=1, tiled=True)
    residual = lax.all_to_all(residual, "tensor", split_axis=0, concat_axis=1, tiled=True)
    inputs = inputs.astype(jnp.float32)
    gain = lax.all_gather(norm_gain, "tensor", axis=0, tiled=True)
    target = targets(img_count, img_dest, groups, capacity)
    target = lax.all_gather(target, "dp", axis=0)

    partial_value = transposed_product(picked, query_weight).astype(jnp.bfloat16)
    partial_value = partial_value.reshape(groups, parts, rows, block)
    summed = lax.psum_scatter(partial_value, "tensor", scatter_dimension=1, tiled=False)
    normal_grad = lax.all_to_all(summed, "dp", split_axis=0, concat_axis=0, tiled=True)
    normal_grad = normal_grad.transpose(1, 0, 2).reshape(rows, width).astype(jnp.float32)

    scaled = gain[None, :] * normal_grad
    squares = jnp.sum(inputs * inputs, axis=1)
    inner_sum = jnp.sum(scaled * inputs, axis=1)
    inverse = lax.rsqrt(squares / width + NORM_EPS)
    handoff = (
        residual.astype(jnp.float32)
        + inverse[:, None] * scaled
        - inputs * (inverse**3 * inner_sum / width)[:, None]
    )
    handoff = handoff.astype(jnp.bfloat16)
    handoff = lax.all_to_all(handoff, "tensor", split_axis=1, concat_axis=0, tiled=True)
    handoff = lax.all_gather(handoff, "dp", axis=0, tiled=True)

    hidden = transposed_product(handoff, merge_weight).astype(jnp.bfloat16)
    hidden_block = hidden.shape[1]
    hidden = hidden.reshape(groups, image_count, hidden_block)
    placing = jnp.arange(groups * capacity, dtype=jnp.int32)[None, :, None] == target[:, None, :]
    placed = jnp.einsum(
        "spj,sjh->sph", placing.astype(jnp.bfloat16), hidden, preferred_element_type=jnp.float32
    ).astype(jnp.bfloat16)
    placed = placed.reshape(groups, groups, capacity, hidden_block).transpose(1, 0, 2, 3)
    placed = placed.reshape(groups, parts, groups * capacity // parts, hidden_block)
    summed = lax.psum_scatter(placed, "tensor", scatter_dimension=1, tiled=False)
    summed = lax.all_to_all(summed, "dp", split_axis=0, concat_axis=0, tiled=True)
    summed = summed.transpose(1, 0, 2).reshape(groups * capacity // parts, groups * hidden_block)
    hidden_grad = lax.all_to_all(summed, "tensor", split_axis=1, concat_axis=0, tiled=True)
    return hidden_grad.astype(jnp.float32) * gelu_slope(merge_pre)


Z = 4
CORES = 2
PARTS = 4
UNIT = 16
TILE = 128
MESH = pl.DeviceIdType.MESH
BF16 = jnp.bfloat16
F32 = jnp.float32


def stage_order(z, step):
    near = jnp.where(z >= 2, Z - 1 - z, z)
    at = jnp.where((near == 1) & (step < 2), 1 - step, step)
    return jnp.where(z >= 2, Z - 1 - at, at)


def remote(src, dst, send, recv, device):
    return pltpu.make_async_remote_copy(
        src_ref=src, dst_ref=dst, send_sem=send, recv_sem=recv, device_id=device, device_id_type=MESH
    )


def fused_kernel(
    capacity,
    gq, pos, count, dest, gain, wq_hbm, em_hbm, gr_hbm, wm_hbm, mp_hbm,
    out,
    wq, em, gr, wm, mp, slope, wq_t, wm_t,
    x, part, part_in, sums, grads,
    em_rows, gr_rows, ng, stat, rows_at,
    h, q, q_in, u, w, f,
    local_sem, x_s, x_r, part_s, part_r, sums_s, grads_r,
    ng_s, ng_r, stat_s, stat_r, at_s, at_r,
    h_s, h_r, q_s, q_r, u_s, w_r, w_s, f_r,
):
    s = lax.axis_index("dp")
    t = lax.axis_index("tensor")
    z = s // CORES
    c = s % CORES
    groups = Z * CORES
    sib = z * CORES + 1 - c
    sibling = (sib, t)
    tokens = gq.shape[0]
    image_count = pos.shape[1]
    half = image_count // 2
    rows = half // PARTS
    block = wq.shape[0]
    width = block * groups
    hidden = wm.shape[0]
    tiles = hidden // TILE
    pair_rows = CORES * capacity
    middle = (z == 1) | (z == 2)

    loads = [
        pltpu.make_async_copy(src, dst, local_sem.at[i])
        for i, (src, dst) in enumerate(
            ((wq_hbm, wq), (em_hbm, em), (gr_hbm, gr), (wm_hbm, wm), (mp_hbm, mp))
        )
    ]
    for load in loads:
        load.start()

    barrier = pltpu.get_barrier_semaphore()
    for k in range(1, groups):
        pl.semaphore_signal(barrier, inc=1, device_id=((s + k) % groups, t), device_id_type=MESH)
    for k in range(1, PARTS):
        pl.semaphore_signal(barrier, inc=1, device_id=(s, (t + k) % PARTS), device_id_type=MESH)

    hot = (lax.broadcasted_iota(jnp.int32, (tokens, image_count), 0) == pos[...]).astype(F32).astype(BF16)

    def pick(ref):
        return lax.dot_general(
            hot, ref[...], (((0,), (0,)), ((), ())), preferred_element_type=F32
        ).astype(BF16)

    x[pl.ds(s, 1)] = pick(gq).reshape(1, 2, half, -1)
    pl.semaphore_wait(barrier, groups - 1 + PARTS - 1)

    def kinds_of(ref, send, recv):
        def make(side, device):
            return lambda b, d: remote(
                ref.at[b, d], ref.at[b, d], send.at[b, d, side], recv.at[b, d], device
            )

        return make(0, (s + CORES, t)), make(1, (s - CORES, t)), make(2, sibling)

    x_kinds = kinds_of(x, x_s, x_r)
    h_kinds = kinds_of(h, h_s, h_r)

    def spread(act, kinds, zz, d):
        b = zz * CORES + c
        right, left, side = kinds

        @pl.when((zz <= z) & (z < Z - 1))
        def _():
            act(right(b, d))

        @pl.when((zz >= z) & (z > 0))
        def _():
            act(left(b, d))

        act(side(b, d))

    def start(copy):
        copy.start()

    def sent(copy):
        copy.wait_send()

    def peer(k):
        return (t + k) % PARTS

    def arrived(ref, sem):
        remote(ref, ref, x_s.at[0, 0, 0], sem, sibling).wait_recv()

    def pass_on(ref, recv, kinds, zz, d):
        b = zz * CORES + c
        arrived(ref.at[b, d], recv.at[b, d])
        spread(start, kinds, zz, d)

    spread(start, x_kinds, z, 0)

    lane = lax.broadcasted_iota(jnp.int32, (groups, image_count), 1)
    hot_dest = (dest[...] == lax.broadcasted_iota(jnp.int32, (groups, image_count), 0)) & (lane < count[0])
    hot_dest = hot_dest.astype(F32)
    before = (
        lax.broadcasted_iota(jnp.int32, (image_count, image_count), 0)
        < lax.broadcasted_iota(jnp.int32, (image_count, image_count), 1)
    ).astype(F32)
    earlier = jnp.dot(hot_dest, before, preferred_element_type=F32)
    slot = jnp.sum(earlier * hot_dest, axis=0, keepdims=True).astype(jnp.int32)
    spot = c * capacity + slot
    at = jnp.where(lane[:1] < count[0], dest[...] * pair_rows + spot, -1)
    rows_at[pl.ds(s, 1)] = jnp.broadcast_to(at, (1, 8, image_count))

    def at_copy(k):
        return remote(rows_at.at[s], rows_at.at[s], at_s.at[k], at_r.at[s], ((s + k) % groups, t))

    for k in range(1, groups):
        at_copy(k).start()

    def part_copy(d, zz, k):
        p = peer(k)
        return remote(
            part.at[d, zz, p], part_in.at[d, zz, t], part_s.at[d, zz, k], part_r.at[d, zz, t], (s, p)
        )

    def sums_copy(d, zz, cc):
        return remote(
            sums.at[d, zz, cc], grads.at[d, s], sums_s.at[d, zz, cc], grads_r.at[d, s],
            (zz * CORES + cc, t),
        )

    def add_parts(g):
        d = g // Z
        zz = stage_order(z, g % Z)
        total = part[d, zz, t].astype(F32)
        for k in range(1, PARTS):
            p = peer(k)
            arrived(part_in.at[d, zz, p], part_r.at[d, zz, p])
            total += part_in[d, zz, p].astype(F32)
        sums[pl.ds(d, 1), pl.ds(zz, 1)] = total.astype(BF16)[None, None]
        for cc in range(CORES):
            own = (zz == z) & (c == cc)

            @pl.when(jnp.logical_not(own))
            def _():
                sums_copy(d, zz, cc).start()

            @pl.when(own)
            def _():
                grads[pl.ds(d, 1), pl.ds(s, 1)] = sums[d, zz, cc][None, None]

    def grad_copy(d, k):
        p = peer(k)
        return remote(
            grads.at[d, pl.ds(p * 2, 2)], ng.at[d, t], ng_s.at[d, k], ng_r.at[d, t], (s, p)
        )

    def norm_send(d):
        for k in range(1, groups):
            b = (s + k) % groups
            arrived(grads.at[d, b], grads_r.at[d, b])
        for k in range(1, PARTS):
            grad_copy(d, k).start()
        ng[d, pl.ds(t, 1)] = grads[d, pl.ds(t * 2, 2)][None]

    def stat_copy(d, k):
        return remote(stat.at[d, t], stat.at[d, t], stat_s.at[d, k], stat_r.at[d, t], (s, peer(k)))

    def pieces(d, p):
        for e in range(2):
            lo = e * block
            top = d * half + p * rows
            value = em_rows[top:top + rows, lo:lo + block].astype(F32)
            yield lo, top, value, gain[:, lo:lo + block] * ng[d, p, e].astype(F32)

    def norm_stats(d):
        for k in range(1, PARTS):
            p = peer(k)
            arrived(ng.at[d, p], ng_r.at[d, p])
        side = lax.broadcasted_iota(jnp.int32, (rows, 128), 1)
        for p in range(PARTS):
            squares = jnp.zeros((rows, 1), F32)
            inner = jnp.zeros((rows, 1), F32)
            for lo, top, value, scaled in pieces(d, p):
                squares += jnp.sum(value * value, axis=1, keepdims=True)
                inner += jnp.sum(scaled * value, axis=1, keepdims=True)
            both = jnp.where(side < 64, squares, inner)
            stat[d, pl.ds(t, 1), p * rows:(p + 1) * rows] = both[None]
        for k in range(1, PARTS):
            stat_copy(d, k).start()

    def norm_finish(d):
        for k in range(1, PARTS):
            p = peer(k)
            arrived(stat.at[d, p], stat_r.at[d, p])
        for p in range(PARTS):
            total = jnp.zeros((rows, 128), F32)
            for src in range(PARTS):
                total += stat[d, src, p * rows:(p + 1) * rows]
            inverse = lax.rsqrt(total[:, 0:1] / width + NORM_EPS)
            back = inverse * inverse * inverse * total[:, 64:65] / width
            for lo, top, value, scaled in pieces(d, p):
                residual = gr_rows[top:top + rows, lo:lo + block].astype(F32)
                result = residual + inverse * scaled - value * back
                h[pl.ds(s, 1), d, p * rows:(p + 1) * rows, lo:lo + block] = result.astype(BF16)[None]
        spread(start, h_kinds, z, d)

    def turn(src, dst):
        for lo in range(0, src.shape[0], TILE):
            dst[:, lo:lo + TILE] = src[lo:lo + TILE].T

    loads[0].wait()
    turn(wq, wq_t)
    pass_on(x, x_r, x_kinds, stage_order(z, 1), 0)

    @pl.when(middle)
    def _():
        pass_on(x, x_r, x_kinds, stage_order(z, 2), 0)

    spread(start, x_kinds, z, 1)

    def first_step(g, carry):
        d, step = g // Z, g % Z
        zz = stage_order(z, step)
        passes = (g == Z + 1) | (step == 3) | ((step == 2) & jnp.logical_not(middle))
        late = (g == 2 * Z - 1) & jnp.logical_not(middle)

        @pl.when(passes & jnp.logical_not(late))
        def _():
            pass_on(x, x_r, x_kinds, zz, d)

        @pl.when((g == Z + 1) & middle)
        def _():
            pass_on(x, x_r, x_kinds, stage_order(z, 2), d)

        @pl.when(g == 2 * Z - 1)
        def _():
            norm_stats(0)

        @pl.when(late)
        def _():
            pass_on(x, x_r, x_kinds, zz, d)

        b = zz * CORES + 1 - c
        arrived(x.at[b, d], x_r.at[b, d])
        left = x[pl.ds(zz * CORES, CORES), pl.ds(d, 1)].reshape(CORES * half, -1)
        tile = 256
        for n in range(0, block, tile):
            piece = jnp.dot(left, wq_t[:, n:n + tile], preferred_element_type=F32).astype(BF16)
            piece = piece.reshape(CORES, PARTS, rows, tile)
            for p in range(PARTS):
                part[pl.ds(d, 1), pl.ds(zz, 1), p, :, :, n:n + tile] = piece[:, p][None, None]
        for k in range(1, PARTS):
            part_copy(d, zz, k).start()

        @pl.when(g == 1)
        def _():
            loads[1].wait()
            em_rows[...] = pick(em)
            loads[2].wait()
            gr_rows[...] = pick(gr)

        @pl.when(g == 2)
        def _():
            loads[3].wait()
            turn(wm, wm_t)

        @pl.when(g == 4)
        def _():
            loads[4].wait()

            def some_rows(i, carry):
                span = pl.ds(pl.multiple_of(i * UNIT, UNIT), UNIT)
                slope[span] = gelu_slope(mp[span])
                return carry

            lax.fori_loop(0, mp.shape[0] // UNIT, some_rows, 0)

        @pl.when(g == 2 * Z - 1)
        def _():
            norm_finish(0)

        @pl.when(g > 0)
        def _():
            add_parts(g - 1)

        @pl.when(g == 2 * Z - 2)
        def _():
            norm_send(0)

        return carry

    lax.fori_loop(0, 2 * Z, first_step, 0)
    add_parts(2 * Z - 1)

    pass_on(h, h_r, h_kinds, stage_order(z, 1), 0)

    @pl.when(middle)
    def _():
        pass_on(h, h_r, h_kinds, stage_order(z, 2), 0)

    norm_send(1)
    norm_stats(1)
    norm_finish(1)

    for k in range(1, groups):
        b = (s + k) % groups
        arrived(rows_at.at[b], at_r.at[b])

    def first_tile(zz):
        return (t + PARTS - zz) % PARTS

    def held(zz, e):
        return (first_tile(zz) == 0) | (e == 0)

    def tile_of(zz, e):
        return first_tile(zz) if e == 0 else PARTS

    def q_copy(zz, d, j):
        e = j // PARTS
        return remote(
            q.at[zz, d, j], q_in.at[zz, d, e, t], q_s.at[zz, d, j], q_r.at[zz, d, e, t],
            (s, (j + zz) % PARTS),
        )

    def u_copy(zz, e, r):
        return remote(u.at[zz, e, r], w.at[s, zz, e], u_s.at[zz, e, r], w_r.at[s, zz, e], (r, t))

    def add_tiles(zz):
        places = []
        for d in range(2):
            lo = d * half
            spots = jnp.concatenate(
                [rows_at[zz * CORES + cc, 0:1, lo:lo + half] for cc in range(CORES)], axis=1
            )
            hot_rows = lax.broadcasted_iota(jnp.int32, (groups * pair_rows, CORES * half), 0) == spots
            places.append(hot_rows.astype(F32).astype(BF16))
        for e in range(2):
            @pl.when(held(zz, e))
            def _():
                placed = jnp.zeros((groups * pair_rows, TILE), F32)
                for d in range(2):
                    total = q[zz, d, tile_of(zz, e)].astype(F32)
                    for k in range(1, PARTS):
                        p = peer(k)
                        arrived(q_in.at[zz, d, e, p], q_r.at[zz, d, e, p])
                        total += q_in[zz, d, e, p].astype(F32)
                    placed += jnp.dot(places[d], total.astype(BF16), preferred_element_type=F32)
                placed = placed.astype(BF16).reshape(1, 1, groups, pair_rows, TILE)
                u[pl.ds(zz, 1), e:e + 1] = placed
                for k in range(1, groups):
                    u_copy(zz, e, (s + k) % groups).start()
                w[pl.ds(s, 1), pl.ds(zz, 1), e] = u[zz, e, s][None, None]

    def second_step(i, carry):
        step, d = i // 2, i % 2
        zz = stage_order(z, step)
        ends = jnp.logical_not(middle)

        @pl.when((i == 3) | ((i > 3) & ends))
        def _():
            pass_on(h, h_r, h_kinds, zz, d)

        @pl.when((i == 3) & middle)
        def _():
            pass_on(h, h_r, h_kinds, stage_order(z, 2), 1)

        b = zz * CORES + 1 - c
        arrived(h.at[b, d], h_r.at[b, d])
        left = h[pl.ds(zz * CORES, CORES), pl.ds(d, 1)].reshape(CORES * half, -1)
        for j in range(0, tiles, 2):
            hi = min(j + 2, tiles)
            piece = jnp.dot(left, wm_t[:, j * TILE:hi * TILE], preferred_element_type=F32).astype(BF16)
            for jj in range(j, hi):
                q[pl.ds(zz, 1), pl.ds(d, 1), jj] = piece[:, (jj - j) * TILE:(jj - j + 1) * TILE][None, None]
        for j in range(tiles):
            @pl.when((j + zz) % PARTS != t)
            def _():
                q_copy(zz, d, j).start()

        @pl.when(((i == 3) | (i == 5)) & middle)
        def _():
            pass_on(h, h_r, h_kinds, stage_order(z, 3), i // 5)

        @pl.when((i > 1) & (d == 0))
        def _():
            add_tiles(stage_order(z, step - 1))

        return carry

    lax.fori_loop(0, 2 * Z, second_step, 0)
    add_tiles(stage_order(z, Z - 1))

    def f_copy(b, zz, e):
        j = tile_of(zz, e)
        return remote(
            w.at[b, zz, e], f.at[zz, b % 2, j], w_s.at[b, zz, e], f_r.at[zz, b % 2, j], (s, b // 2)
        )

    def hand_out(i, carry):
        step, k = i // groups, i % groups
        b = (s + k) % groups
        zz = stage_order(b // CORES, step)
        for e in range(2):
            @pl.when(held(zz, e))
            def _():
                @pl.when(b != s)
                def _():
                    arrived(w.at[b, zz, e], w_r.at[b, zz, e])

                @pl.when(b // 2 != t)
                def _():
                    f_copy(b, zz, e).start()

                @pl.when(b // 2 == t)
                def _():
                    f[pl.ds(zz, 1), pl.ds(b % 2, 1), pl.ds(tile_of(zz, e), 1)] = w[b, zz, e][None, None, None]

        return carry

    lax.fori_loop(0, Z * groups, hand_out, 0)

    def finish(zz, carry):
        span = pl.ds(pl.multiple_of(zz * pair_rows, pair_rows), pair_rows)
        for side in range(2):
            for j in range(tiles):
                @pl.when((j + zz) % PARTS != t)
                def _():
                    arrived(f.at[zz, side, j], f_r.at[zz, side, j])

                lo = side * hidden + j * TILE
                out[span, lo:lo + TILE] = f[zz, side, j].astype(F32) * slope[span, lo:lo + TILE]
        return carry

    lax.fori_loop(0, Z, finish, 0)

    for k in range(1, groups):
        sent(at_copy(k))
    for d in range(2):
        for k in range(1, PARTS):
            sent(grad_copy(d, k))
            sent(stat_copy(d, k))

    def all_sent(zz, carry):
        for d in range(2):
            spread(sent, x_kinds, zz, d)
            spread(sent, h_kinds, zz, d)
            for k in range(1, PARTS):
                sent(part_copy(d, zz, k))
            for cc in range(CORES):
                @pl.when((zz != z) | (c != cc))
                def _():
                    sent(sums_copy(d, zz, cc))

        for j in range(tiles):
            @pl.when((j + zz) % PARTS != t)
            def _():
                for d in range(2):
                    sent(q_copy(zz, d, j))

        for e in range(2):
            @pl.when(held(zz, e))
            def _():
                for k in range(1, groups):
                    sent(u_copy(zz, e, (s + k) % groups))
                for b in range(groups):
                    @pl.when(b // 2 != t)
                    def _():
                        sent(f_copy(b, zz, e))

        return carry

    lax.fori_loop(0, Z, all_sent, 0)


def fused(grad_query, query_weight, grad_resid, embeds, norm_gain, img_pos, img_count, img_dest, merge_weight, merge_pre):
    groups = Z * CORES
    capacity = merge_pre.shape[0] // groups
    image_count = img_pos.shape[1]
    half = image_count // 2
    rows = half // PARTS
    block, columns = query_weight.shape
    tiles = merge_weight.shape[0] // TILE
    pair_rows = CORES * capacity
    vmem = pltpu.VMEM
    dma = pltpu.SemaphoreType.DMA
    in_vmem = pl.BlockSpec(memory_space=pltpu.VMEM)
    anywhere = pl.BlockSpec(memory_space=pl.ANY)
    scratch = [
        vmem(query_weight.shape, BF16), vmem(embeds.shape, BF16), vmem(grad_resid.shape, BF16),
        vmem(merge_weight.shape, BF16), vmem(merge_pre.shape, BF16), vmem(merge_pre.shape, F32),
        vmem(query_weight.shape[::-1], BF16), vmem(merge_weight.shape[::-1], BF16),
        vmem((groups, 2, half, columns), BF16),
        vmem((2, Z, PARTS, CORES, rows, block), BF16), vmem((2, Z, PARTS, CORES, rows, block), BF16),
        vmem((2, Z, CORES, rows, block), BF16), vmem((2, groups, rows, block), BF16),
        vmem((image_count, columns), BF16), vmem((image_count, columns), BF16),
        vmem((2, PARTS, 2, rows, block), BF16), vmem((2, PARTS, half, 128), F32),
        vmem((groups, 8, image_count), jnp.int32),
        vmem((groups, 2, half, columns), BF16),
        vmem((Z, 2, tiles, CORES * half, TILE), BF16), vmem((Z, 2, 2, PARTS, CORES * half, TILE), BF16),
        vmem((Z, 2, groups, pair_rows, TILE), BF16), vmem((groups, Z, 2, pair_rows, TILE), BF16),
        vmem((Z, 2, tiles, pair_rows, TILE), BF16),
        dma((5,)), dma((groups, 2, 3)), dma((groups, 2)), dma((2, Z, PARTS)), dma((2, Z, PARTS)),
        dma((2, Z, CORES)), dma((2, groups)),
        dma((2, PARTS)), dma((2, PARTS)), dma((2, PARTS)), dma((2, PARTS)), dma((groups,)), dma((groups,)),
        dma((groups, 2, 3)), dma((groups, 2)), dma((Z, 2, tiles)), dma((Z, 2, 2, PARTS)),
        dma((Z, 2, groups)), dma((groups, Z, 2)), dma((groups, Z, 2)), dma((Z, 2, tiles)),
    ]
    return pl.pallas_call(
        functools.partial(fused_kernel, capacity),
        out_shape=jax.ShapeDtypeStruct(merge_pre.shape, F32),
        in_specs=[
            in_vmem, in_vmem, pl.BlockSpec(memory_space=pltpu.SMEM), in_vmem, in_vmem,
            anywhere, anywhere, anywhere, anywhere, anywhere,
        ],
        out_specs=in_vmem,
        scratch_shapes=scratch,
        compiler_params=pltpu.CompilerParams(
            collective_id=0, has_side_effects=True, vmem_limit_bytes=56 * 1024 * 1024
        ),
        cost_estimate=pl.CostEstimate(
            flops=4 * groups * image_count * columns * (block + merge_weight.shape[0]),
            bytes_accessed=16 * 1024 * 1024,
            transcendentals=merge_pre.size,
        ),
    )(
        grad_query, img_pos, img_count, img_dest, norm_gain.reshape(1, -1),
        query_weight, embeds, grad_resid, merge_weight, merge_pre,
    )


def solution(mesh):
    in_specs = (
        P("dp", "tensor"),
        P("dp", "tensor"),
        P("dp", "tensor"),
        P("dp", "tensor"),
        P("tensor"),
        P("dp", None),
        P("dp"),
        P("dp", None),
        P("dp", "tensor"),
        P("dp", "tensor"),
    )
    out_specs = P("dp", "tensor")
    known = mesh.shape["dp"] == Z * CORES and mesh.shape["tensor"] == PARTS
    body = fused if known else local
    return jax.shard_map(body, mesh=mesh, in_specs=in_specs, out_specs=out_specs, check_vma=False)
```

```python
import functools

import jax
import jax.numpy as jnp
from jax import lax
from jax.experimental import pallas as pl
from jax.experimental.pallas import tpu as pltpu
from jax.sharding import PartitionSpec as P

NORM_EPS = 1e-06


def gelu_slope(pre):
    value = pre.astype(jnp.float32)
    cdf_part = 0.5 * (1.0 + lax.erf(value * 0.7071067811865476))
    pdf_part = jnp.exp(-0.5 * value * value) * 0.3989422804014327
    return cdf_part + value * pdf_part


def transposed_product(left, right):
    return lax.dot_general(
        left, right, (((1,), (1,)), ((), ())), preferred_element_type=jnp.float32
    )


def targets(img_count, img_dest, groups, capacity):
    image_count = img_dest.shape[1]
    is_live = jnp.arange(image_count, dtype=jnp.int32) < img_count[0]
    target_dev = img_dest[0]
    dest_hot = (
        (target_dev[:, None] == jnp.arange(groups, dtype=jnp.int32)[None, :]) & is_live[:, None]
    ).astype(jnp.int32)
    earlier = jnp.cumsum(dest_hot, axis=0) - dest_hot
    slot_index = jnp.sum(earlier * dest_hot, axis=1)
    return jnp.where(is_live, target_dev * capacity + slot_index, -1)


def local(
    grad_query,
    query_weight,
    grad_resid,
    embeds,
    norm_gain,
    img_pos,
    img_count,
    img_dest,
    merge_weight,
    merge_pre,
):
    groups = lax.axis_size("dp")
    parts = lax.axis_size("tensor")
    capacity = merge_pre.shape[0] // groups
    positions = img_pos[0]
    image_count = positions.shape[0]
    rows = image_count // parts
    block = query_weight.shape[0]
    width = block * groups
    picked = lax.all_gather(jnp.take(grad_query, positions, axis=0), "dp", axis=0, tiled=True)
    inputs = jnp.take(embeds, positions, axis=0)
    residual = jnp.take(grad_resid, positions, axis=0)
    inputs = lax.all_to_all(inputs, "tensor", split_axis=0, concat_axis=1, tiled=True)
    residual = lax.all_to_all(residual, "tensor", split_axis=0, concat_axis=1, tiled=True)
    inputs = inputs.astype(jnp.float32)
    gain = lax.all_gather(norm_gain, "tensor", axis=0, tiled=True)
    target = targets(img_count, img_dest, groups, capacity)
    target = lax.all_gather(target, "dp", axis=0)

    partial_value = transposed_product(picked, query_weight).astype(jnp.bfloat16)
    partial_value = partial_value.reshape(groups, parts, rows, block)
    summed = lax.psum_scatter(partial_value, "tensor", scatter_dimension=1, tiled=False)
    normal_grad = lax.all_to_all(summed, "dp", split_axis=0, concat_axis=0, tiled=True)
    normal_grad = normal_grad.transpose(1, 0, 2).reshape(rows, width).astype(jnp.float32)

    scaled = gain[None, :] * normal_grad
    squares = jnp.sum(inputs * inputs, axis=1)
    inner_sum = jnp.sum(scaled * inputs, axis=1)
    inverse = lax.rsqrt(squares / width + NORM_EPS)
    handoff = (
        residual.astype(jnp.float32)
        + inverse[:, None] * scaled
        - inputs * (inverse**3 * inner_sum / width)[:, None]
    )
    handoff = handoff.astype(jnp.bfloat16)
    handoff = lax.all_to_all(handoff, "tensor", split_axis=1, concat_axis=0, tiled=True)
    handoff = lax.all_gather(handoff, "dp", axis=0, tiled=True)

    hidden = transposed_product(handoff, merge_weight).astype(jnp.bfloat16)
    hidden_block = hidden.shape[1]
    hidden = hidden.reshape(groups, image_count, hidden_block)
    placing = jnp.arange(groups * capacity, dtype=jnp.int32)[None, :, None] == target[:, None, :]
    placed = jnp.einsum(
        "spj,sjh->sph", placing.astype(jnp.bfloat16), hidden, preferred_element_type=jnp.float32
    ).astype(jnp.bfloat16)
    placed = placed.reshape(groups, groups, capacity, hidden_block).transpose(1, 0, 2, 3)
    placed = placed.reshape(groups, parts, groups * capacity // parts, hidden_block)
    summed = lax.psum_scatter(placed, "tensor", scatter_dimension=1, tiled=False)
    summed = lax.all_to_all(summed, "dp", split_axis=0, concat_axis=0, tiled=True)
    summed = summed.transpose(1, 0, 2).reshape(groups * capacity // parts, groups * hidden_block)
    hidden_grad = lax.all_to_all(summed, "tensor", split_axis=1, concat_axis=0, tiled=True)
    return hidden_grad.astype(jnp.float32) * gelu_slope(merge_pre)


Z = 4
CORES = 2
PARTS = 4
UNIT = 16
TILE = 128
MESH = pl.DeviceIdType.MESH
BF16 = jnp.bfloat16
F32 = jnp.float32


def stage_order(z, step):
    near = jnp.where(z >= 2, Z - 1 - z, z)
    at = jnp.where((near == 1) & (step < 3), (step + 1) % 3, step)
    return jnp.where(z >= 2, Z - 1 - at, at)


def remote(src, dst, send, recv, device):
    return pltpu.make_async_remote_copy(
        src_ref=src, dst_ref=dst, send_sem=send, recv_sem=recv, device_id=device, device_id_type=MESH
    )


def fused_kernel(
    capacity,
    gq, pos, count, dest, gain, wq_hbm, em_hbm, gr_hbm, wm_hbm, mp_hbm,
    out,
    wq, em, gr, wm, mp, slope, wq_t, wm_t,
    x, part, part_in, sums, grads,
    em_rows, gr_rows, ng, stat, rows_at,
    h, q, q_in, u, w, f,
    local_sem, x_s, x_r, part_s, part_r, sums_s, grads_r,
    ng_s, ng_r, stat_s, stat_r, at_s, at_r,
    h_s, h_r, q_s, q_r, u_s, w_r, w_s, f_r,
):
    s = lax.axis_index("dp")
    t = lax.axis_index("tensor")
    z = s // CORES
    c = s % CORES
    groups = Z * CORES
    sib = z * CORES + 1 - c
    sibling = (sib, t)
    tokens = gq.shape[0]
    image_count = pos.shape[1]
    half = image_count // 2
    rows = half // PARTS
    block = wq.shape[0]
    width = block * groups
    hidden = wm.shape[0]
    tiles = hidden // TILE
    pair_rows = CORES * capacity
    middle = (z == 1) | (z == 2)

    loads = [
        pltpu.make_async_copy(src, dst, local_sem.at[i])
        for i, (src, dst) in enumerate(
            ((wq_hbm, wq), (em_hbm, em), (gr_hbm, gr), (wm_hbm, wm), (mp_hbm, mp))
        )
    ]
    for load in loads:
        load.start()

    barrier = pltpu.get_barrier_semaphore()
    for k in range(1, groups):
        pl.semaphore_signal(barrier, inc=1, device_id=((s + k) % groups, t), device_id_type=MESH)
    for k in range(1, PARTS):
        pl.semaphore_signal(barrier, inc=1, device_id=(s, (t + k) % PARTS), device_id_type=MESH)

    hot = (lax.broadcasted_iota(jnp.int32, (tokens, image_count), 0) == pos[...]).astype(F32).astype(BF16)

    def pick(ref):
        return lax.dot_general(
            hot, ref[...], (((0,), (0,)), ((), ())), preferred_element_type=F32
        ).astype(BF16)

    x[pl.ds(s, 1)] = pick(gq).reshape(1, 2, half, -1)
    pl.semaphore_wait(barrier, groups - 1 + PARTS - 1)

    def kinds_of(ref, send, recv):
        def make(side, device):
            return lambda b, d: remote(
                ref.at[b, d], ref.at[b, d], send.at[b, d, side], recv.at[b, d], device
            )

        return make(0, (s + CORES, t)), make(1, (s - CORES, t)), make(2, sibling)

    x_kinds = kinds_of(x, x_s, x_r)
    h_kinds = kinds_of(h, h_s, h_r)

    def spread(act, kinds, zz, d):
        b = zz * CORES + c
        right, left, side = kinds

        @pl.when((zz <= z) & (z < Z - 1))
        def _():
            act(right(b, d))

        @pl.when((zz >= z) & (z > 0))
        def _():
            act(left(b, d))

        act(side(b, d))

    def start(copy):
        copy.start()

    def sent(copy):
        copy.wait_send()

    def peer(k):
        return (t + k) % PARTS

    def arrived(ref, sem):
        remote(ref, ref, x_s.at[0, 0, 0], sem, sibling).wait_recv()

    def pass_on(ref, recv, kinds, zz, d):
        b = zz * CORES + c
        arrived(ref.at[b, d], recv.at[b, d])
        spread(start, kinds, zz, d)

    spread(start, x_kinds, z, 0)

    lane = lax.broadcasted_iota(jnp.int32, (groups, image_count), 1)
    hot_dest = (dest[...] == lax.broadcasted_iota(jnp.int32, (groups, image_count), 0)) & (lane < count[0])
    hot_dest = hot_dest.astype(F32)
    before = (
        lax.broadcasted_iota(jnp.int32, (image_count, image_count), 0)
        < lax.broadcasted_iota(jnp.int32, (image_count, image_count), 1)
    ).astype(F32)
    earlier = jnp.dot(hot_dest, before, preferred_element_type=F32)
    slot = jnp.sum(earlier * hot_dest, axis=0, keepdims=True).astype(jnp.int32)
    spot = c * capacity + slot
    at = jnp.where(lane[:1] < count[0], dest[...] * pair_rows + spot, -1)
    rows_at[pl.ds(s, 1)] = jnp.broadcast_to(at, (1, 8, image_count))

    def at_copy(k):
        return remote(rows_at.at[s], rows_at.at[s], at_s.at[k], at_r.at[s], ((s + k) % groups, t))

    for k in range(1, groups):
        at_copy(k).start()

    def part_copy(d, zz, k):
        p = peer(k)
        return remote(
            part.at[d, zz, p], part_in.at[d, zz, t], part_s.at[d, zz, k], part_r.at[d, zz, t], (s, p)
        )

    def sums_copy(d, zz, cc):
        return remote(
            sums.at[d, zz, cc], grads.at[d, s], sums_s.at[d, zz, cc], grads_r.at[d, s],
            (zz * CORES + cc, t),
        )

    def add_parts(g):
        d = g // Z
        zz = stage_order(z, g % Z)
        total = part[d, zz, t].astype(F32)
        for k in range(1, PARTS):
            p = peer(k)
            arrived(part_in.at[d, zz, p], part_r.at[d, zz, p])
            total += part_in[d, zz, p].astype(F32)
        sums[pl.ds(d, 1), pl.ds(zz, 1)] = total.astype(BF16)[None, None]
        for cc in range(CORES):
            own = (zz == z) & (c == cc)

            @pl.when(jnp.logical_not(own))
            def _():
                sums_copy(d, zz, cc).start()

            @pl.when(own)
            def _():
                grads[pl.ds(d, 1), pl.ds(s, 1)] = sums[d, zz, cc][None, None]

    def grad_copy(d, k):
        p = peer(k)
        return remote(
            grads.at[d, pl.ds(p * 2, 2)], ng.at[d, t], ng_s.at[d, k], ng_r.at[d, t], (s, p)
        )

    def norm_send(d):
        for k in range(1, groups):
            b = (s + k) % groups
            arrived(grads.at[d, b], grads_r.at[d, b])
        for k in range(1, PARTS):
            grad_copy(d, k).start()
        ng[d, pl.ds(t, 1)] = grads[d, pl.ds(t * 2, 2)][None]

    def stat_copy(d, k):
        return remote(stat.at[d, t], stat.at[d, t], stat_s.at[d, k], stat_r.at[d, t], (s, peer(k)))

    def pieces(d, p):
        for e in range(2):
            lo = e * block
            top = d * half + p * rows
            value = em_rows[top:top + rows, lo:lo + block].astype(F32)
            yield lo, top, value, gain[:, lo:lo + block] * ng[d, p, e].astype(F32)

    def norm_stats(d):
        for k in range(1, PARTS):
            p = peer(k)
            arrived(ng.at[d, p], ng_r.at[d, p])
        side = lax.broadcasted_iota(jnp.int32, (rows, 128), 1)
        for p in range(PARTS):
            squares = jnp.zeros((rows, 1), F32)
            inner = jnp.zeros((rows, 1), F32)
            for lo, top, value, scaled in pieces(d, p):
                squares += jnp.sum(value * value, axis=1, keepdims=True)
                inner += jnp.sum(scaled * value, axis=1, keepdims=True)
            both = jnp.where(side < 64, squares, inner)
            stat[d, pl.ds(t, 1), p * rows:(p + 1) * rows] = both[None]
        for k in range(1, PARTS):
            stat_copy(d, k).start()

    def norm_finish(d):
        for k in range(1, PARTS):
            p = peer(k)
            arrived(stat.at[d, p], stat_r.at[d, p])
        for p in range(PARTS):
            total = jnp.zeros((rows, 128), F32)
            for src in range(PARTS):
                total += stat[d, src, p * rows:(p + 1) * rows]
            inverse = lax.rsqrt(total[:, 0:1] / width + NORM_EPS)
            back = inverse * inverse * inverse * total[:, 64:65] / width
            for lo, top, value, scaled in pieces(d, p):
                residual = gr_rows[top:top + rows, lo:lo + block].astype(F32)
                result = residual + inverse * scaled - value * back
                h[pl.ds(s, 1), d, p * rows:(p + 1) * rows, lo:lo + block] = result.astype(BF16)[None]
        spread(start, h_kinds, z, d)

    def turn(src, dst):
        for lo in range(0, src.shape[0], TILE):
            dst[:, lo:lo + TILE] = src[lo:lo + TILE].T

    loads[0].wait()
    turn(wq, wq_t)
    pass_on(x, x_r, x_kinds, stage_order(z, 1), 0)

    @pl.when(middle)
    def _():
        pass_on(x, x_r, x_kinds, stage_order(z, 2), 0)

    spread(start, x_kinds, z, 1)

    def first_step(g, carry):
        d, step = g // Z, g % Z
        zz = stage_order(z, step)
        passes = (g == Z + 1) | (step == 3) | ((step == 2) & jnp.logical_not(middle))
        late = (g == 2 * Z - 1) & jnp.logical_not(middle)

        @pl.when(passes & jnp.logical_not(late))
        def _():
            pass_on(x, x_r, x_kinds, zz, d)

        @pl.when((g == Z + 1) & middle)
        def _():
            pass_on(x, x_r, x_kinds, stage_order(z, 2), d)

        @pl.when(g == 2 * Z - 1)
        def _():
            norm_stats(0)

        @pl.when(late)
        def _():
            pass_on(x, x_r, x_kinds, zz, d)

        b = zz * CORES + 1 - c
        arrived(x.at[b, d], x_r.at[b, d])
        left = x[pl.ds(zz * CORES, CORES), pl.ds(d, 1)].reshape(CORES * half, -1)
        tile = 256
        for n in range(0, block, tile):
            piece = jnp.dot(left, wq_t[:, n:n + tile], preferred_element_type=F32).astype(BF16)
            piece = piece.reshape(CORES, PARTS, rows, tile)
            for p in range(PARTS):
                part[pl.ds(d, 1), pl.ds(zz, 1), p, :, :, n:n + tile] = piece[:, p][None, None]
        for k in range(1, PARTS):
            part_copy(d, zz, k).start()

        @pl.when(g == 1)
        def _():
            loads[1].wait()
            em_rows[...] = pick(em)
            loads[2].wait()
            gr_rows[...] = pick(gr)

        @pl.when(g == 2)
        def _():
            loads[3].wait()
            turn(wm, wm_t)

        @pl.when(g == 4)
        def _():
            loads[4].wait()

            def some_rows(i, carry):
                span = pl.ds(pl.multiple_of(i * UNIT, UNIT), UNIT)
                slope[span] = gelu_slope(mp[span])
                return carry

            lax.fori_loop(0, mp.shape[0] // UNIT, some_rows, 0)

        @pl.when(g == 2 * Z - 1)
        def _():
            norm_finish(0)

        @pl.when(g > 0)
        def _():
            add_parts(g - 1)

        @pl.when(g == 2 * Z - 2)
        def _():
            norm_send(0)

        return carry

    lax.fori_loop(0, 2 * Z, first_step, 0)
    add_parts(2 * Z - 1)

    pass_on(h, h_r, h_kinds, stage_order(z, 1), 0)
    norm_send(1)
    norm_stats(1)
    norm_finish(1)

    for k in range(1, groups):
        b = (s + k) % groups
        arrived(rows_at.at[b], at_r.at[b])

    def first_tile(zz):
        return (t + PARTS - zz) % PARTS

    def held(zz, e):
        return (first_tile(zz) == 0) | (e == 0)

    def tile_of(zz, e):
        return first_tile(zz) if e == 0 else PARTS

    def q_copy(zz, d, j):
        e = j // PARTS
        return remote(
            q.at[zz, d, j], q_in.at[zz, d, e, t], q_s.at[zz, d, j], q_r.at[zz, d, e, t],
            (s, (j + zz) % PARTS),
        )

    def u_copy(zz, e, r):
        return remote(u.at[zz, e, r], w.at[s, zz, e], u_s.at[zz, e, r], w_r.at[s, zz, e], (r, t))

    def add_tiles(zz):
        places = []
        for d in range(2):
            lo = d * half
            spots = jnp.concatenate(
                [rows_at[zz * CORES + cc, 0:1, lo:lo + half] for cc in range(CORES)], axis=1
            )
            hot_rows = lax.broadcasted_iota(jnp.int32, (groups * pair_rows, CORES * half), 0) == spots
            places.append(hot_rows.astype(F32).astype(BF16))
        for e in range(2):
            @pl.when(held(zz, e))
            def _():
                placed = jnp.zeros((groups * pair_rows, TILE), F32)
                for d in range(2):
                    total = q[zz, d, tile_of(zz, e)].astype(F32)
                    for k in range(1, PARTS):
                        p = peer(k)
                        arrived(q_in.at[zz, d, e, p], q_r.at[zz, d, e, p])
                        total += q_in[zz, d, e, p].astype(F32)
                    placed += jnp.dot(places[d], total.astype(BF16), preferred_element_type=F32)
                placed = placed.astype(BF16).reshape(1, 1, groups, pair_rows, TILE)
                u[pl.ds(zz, 1), e:e + 1] = placed
                for k in range(1, groups):
                    u_copy(zz, e, (s + k) % groups).start()
                w[pl.ds(s, 1), pl.ds(zz, 1), e] = u[zz, e, s][None, None]

    def second_step(i, carry):
        step, d = i // 2, i % 2
        zz = stage_order(z, step)
        ends = jnp.logical_not(middle)

        @pl.when((i >= 3) & (ends | (i < 6)))
        def _():
            pass_on(h, h_r, h_kinds, zz, d)

        b = zz * CORES + 1 - c
        arrived(h.at[b, d], h_r.at[b, d])
        left = h[pl.ds(zz * CORES, CORES), pl.ds(d, 1)].reshape(CORES * half, -1)
        for j in range(0, tiles, 2):
            hi = min(j + 2, tiles)
            piece = jnp.dot(left, wm_t[:, j * TILE:hi * TILE], preferred_element_type=F32).astype(BF16)
            for jj in range(j, hi):
                q[pl.ds(zz, 1), pl.ds(d, 1), jj] = piece[:, (jj - j) * TILE:(jj - j + 1) * TILE][None, None]
        for j in range(tiles):
            @pl.when((j + zz) % PARTS != t)
            def _():
                q_copy(zz, d, j).start()

        @pl.when(((i == 4) | (i == 5)) & middle)
        def _():
            pass_on(h, h_r, h_kinds, stage_order(z, 3), d)

        @pl.when((i > 1) & (d == 0))
        def _():
            add_tiles(stage_order(z, step - 1))

        return carry

    lax.fori_loop(0, 2 * Z, second_step, 0)
    add_tiles(stage_order(z, Z - 1))

    def f_copy(b, zz, e):
        j = tile_of(zz, e)
        return remote(
            w.at[b, zz, e], f.at[zz, b % 2, j], w_s.at[b, zz, e], f_r.at[zz, b % 2, j], (s, b // 2)
        )

    def hand_out(i, carry):
        step, k = i // groups, i % groups
        b = (s + k) % groups
        zz = stage_order(b // CORES, step)
        for e in range(2):
            @pl.when(held(zz, e))
            def _():
                @pl.when(b != s)
                def _():
                    arrived(w.at[b, zz, e], w_r.at[b, zz, e])

                @pl.when(b // 2 != t)
                def _():
                    f_copy(b, zz, e).start()

                @pl.when(b // 2 == t)
                def _():
                    f[pl.ds(zz, 1), pl.ds(b % 2, 1), pl.ds(tile_of(zz, e), 1)] = w[b, zz, e][None, None, None]

        return carry

    lax.fori_loop(0, Z * groups, hand_out, 0)

    def finish(zz, carry):
        span = pl.ds(pl.multiple_of(zz * pair_rows, pair_rows), pair_rows)
        for side in range(2):
            for j in range(tiles):
                @pl.when((j + zz) % PARTS != t)
                def _():
                    arrived(f.at[zz, side, j], f_r.at[zz, side, j])

                lo = side * hidden + j * TILE
                out[span, lo:lo + TILE] = f[zz, side, j].astype(F32) * slope[span, lo:lo + TILE]
        return carry

    lax.fori_loop(0, Z, finish, 0)

    for k in range(1, groups):
        sent(at_copy(k))
    for d in range(2):
        for k in range(1, PARTS):
            sent(grad_copy(d, k))
            sent(stat_copy(d, k))

    def all_sent(zz, carry):
        for d in range(2):
            spread(sent, x_kinds, zz, d)
            spread(sent, h_kinds, zz, d)
            for k in range(1, PARTS):
                sent(part_copy(d, zz, k))
            for cc in range(CORES):
                @pl.when((zz != z) | (c != cc))
                def _():
                    sent(sums_copy(d, zz, cc))

        for j in range(tiles):
            @pl.when((j + zz) % PARTS != t)
            def _():
                for d in range(2):
                    sent(q_copy(zz, d, j))

        for e in range(2):
            @pl.when(held(zz, e))
            def _():
                for k in range(1, groups):
                    sent(u_copy(zz, e, (s + k) % groups))
                for b in range(groups):
                    @pl.when(b // 2 != t)
                    def _():
                        sent(f_copy(b, zz, e))

        return carry

    lax.fori_loop(0, Z, all_sent, 0)


def fused(grad_query, query_weight, grad_resid, embeds, norm_gain, img_pos, img_count, img_dest, merge_weight, merge_pre):
    groups = Z * CORES
    capacity = merge_pre.shape[0] // groups
    image_count = img_pos.shape[1]
    half = image_count // 2
    rows = half // PARTS
    block, columns = query_weight.shape
    tiles = merge_weight.shape[0] // TILE
    pair_rows = CORES * capacity
    vmem = pltpu.VMEM
    dma = pltpu.SemaphoreType.DMA
    in_vmem = pl.BlockSpec(memory_space=pltpu.VMEM)
    anywhere = pl.BlockSpec(memory_space=pl.ANY)
    scratch = [
        vmem(query_weight.shape, BF16), vmem(embeds.shape, BF16), vmem(grad_resid.shape, BF16),
        vmem(merge_weight.shape, BF16), vmem(merge_pre.shape, BF16), vmem(merge_pre.shape, F32),
        vmem(query_weight.shape[::-1], BF16), vmem(merge_weight.shape[::-1], BF16),
        vmem((groups, 2, half, columns), BF16),
        vmem((2, Z, PARTS, CORES, rows, block), BF16), vmem((2, Z, PARTS, CORES, rows, block), BF16),
        vmem((2, Z, CORES, rows, block), BF16), vmem((2, groups, rows, block), BF16),
        vmem((image_count, columns), BF16), vmem((image_count, columns), BF16),
        vmem((2, PARTS, 2, rows, block), BF16), vmem((2, PARTS, half, 128), F32),
        vmem((groups, 8, image_count), jnp.int32),
        vmem((groups, 2, half, columns), BF16),
        vmem((Z, 2, tiles, CORES * half, TILE), BF16), vmem((Z, 2, 2, PARTS, CORES * half, TILE), BF16),
        vmem((Z, 2, groups, pair_rows, TILE), BF16), vmem((groups, Z, 2, pair_rows, TILE), BF16),
        vmem((Z, 2, tiles, pair_rows, TILE), BF16),
        dma((5,)), dma((groups, 2, 3)), dma((groups, 2)), dma((2, Z, PARTS)), dma((2, Z, PARTS)),
        dma((2, Z, CORES)), dma((2, groups)),
        dma((2, PARTS)), dma((2, PARTS)), dma((2, PARTS)), dma((2, PARTS)), dma((groups,)), dma((groups,)),
        dma((groups, 2, 3)), dma((groups, 2)), dma((Z, 2, tiles)), dma((Z, 2, 2, PARTS)),
        dma((Z, 2, groups)), dma((groups, Z, 2)), dma((groups, Z, 2)), dma((Z, 2, tiles)),
    ]
    return pl.pallas_call(
        functools.partial(fused_kernel, capacity),
        out_shape=jax.ShapeDtypeStruct(merge_pre.shape, F32),
        in_specs=[
            in_vmem, in_vmem, pl.BlockSpec(memory_space=pltpu.SMEM), in_vmem, in_vmem,
            anywhere, anywhere, anywhere, anywhere, anywhere,
        ],
        out_specs=in_vmem,
        scratch_shapes=scratch,
        compiler_params=pltpu.CompilerParams(
            collective_id=0, has_side_effects=True, vmem_limit_bytes=56 * 1024 * 1024
        ),
        cost_estimate=pl.CostEstimate(
            flops=4 * groups * image_count * columns * (block + merge_weight.shape[0]),
            bytes_accessed=16 * 1024 * 1024,
            transcendentals=merge_pre.size,
        ),
    )(
        grad_query, img_pos, img_count, img_dest, norm_gain.reshape(1, -1),
        query_weight, embeds, grad_resid, merge_weight, merge_pre,
    )


def solution(mesh):
    in_specs = (
        P("dp", "tensor"),
        P("dp", "tensor"),
        P("dp", "tensor"),
        P("dp", "tensor"),
        P("tensor"),
        P("dp", None),
        P("dp"),
        P("dp", None),
        P("dp", "tensor"),
        P("dp", "tensor"),
    )
    out_specs = P("dp", "tensor")
    known = mesh.shape["dp"] == Z * CORES and mesh.shape["tensor"] == PARTS
    body = fused if known else local
    return jax.shard_map(body, mesh=mesh, in_specs=in_specs, out_specs=out_specs, check_vma=False)
```

```python
import functools

import jax
import jax.numpy as jnp
from jax import lax
from jax.experimental import pallas as pl
from jax.experimental.pallas import tpu as pltpu
from jax.sharding import PartitionSpec as P

NORM_EPS = 1e-06


def gelu_slope(pre):
    value = pre.astype(jnp.float32)
    cdf_part = 0.5 * (1.0 + lax.erf(value * 0.7071067811865476))
    pdf_part = jnp.exp(-0.5 * value * value) * 0.3989422804014327
    return cdf_part + value * pdf_part


def transposed_product(left, right):
    return lax.dot_general(
        left, right, (((1,), (1,)), ((), ())), preferred_element_type=jnp.float32
    )


def targets(img_count, img_dest, groups, capacity):
    image_count = img_dest.shape[1]
    is_live = jnp.arange(image_count, dtype=jnp.int32) < img_count[0]
    target_dev = img_dest[0]
    dest_hot = (
        (target_dev[:, None] == jnp.arange(groups, dtype=jnp.int32)[None, :]) & is_live[:, None]
    ).astype(jnp.int32)
    earlier = jnp.cumsum(dest_hot, axis=0) - dest_hot
    slot_index = jnp.sum(earlier * dest_hot, axis=1)
    return jnp.where(is_live, target_dev * capacity + slot_index, -1)


def local(
    grad_query,
    query_weight,
    grad_resid,
    embeds,
    norm_gain,
    img_pos,
    img_count,
    img_dest,
    merge_weight,
    merge_pre,
):
    groups = lax.axis_size("dp")
    parts = lax.axis_size("tensor")
    capacity = merge_pre.shape[0] // groups
    positions = img_pos[0]
    image_count = positions.shape[0]
    rows = image_count // parts
    block = query_weight.shape[0]
    width = block * groups
    picked = lax.all_gather(jnp.take(grad_query, positions, axis=0), "dp", axis=0, tiled=True)
    inputs = jnp.take(embeds, positions, axis=0)
    residual = jnp.take(grad_resid, positions, axis=0)
    inputs = lax.all_to_all(inputs, "tensor", split_axis=0, concat_axis=1, tiled=True)
    residual = lax.all_to_all(residual, "tensor", split_axis=0, concat_axis=1, tiled=True)
    inputs = inputs.astype(jnp.float32)
    gain = lax.all_gather(norm_gain, "tensor", axis=0, tiled=True)
    target = targets(img_count, img_dest, groups, capacity)
    target = lax.all_gather(target, "dp", axis=0)

    partial_value = transposed_product(picked, query_weight).astype(jnp.bfloat16)
    partial_value = partial_value.reshape(groups, parts, rows, block)
    summed = lax.psum_scatter(partial_value, "tensor", scatter_dimension=1, tiled=False)
    normal_grad = lax.all_to_all(summed, "dp", split_axis=0, concat_axis=0, tiled=True)
    normal_grad = normal_grad.transpose(1, 0, 2).reshape(rows, width).astype(jnp.float32)

    scaled = gain[None, :] * normal_grad
    squares = jnp.sum(inputs * inputs, axis=1)
    inner_sum = jnp.sum(scaled * inputs, axis=1)
    inverse = lax.rsqrt(squares / width + NORM_EPS)
    handoff = (
        residual.astype(jnp.float32)
        + inverse[:, None] * scaled
        - inputs * (inverse**3 * inner_sum / width)[:, None]
    )
    handoff = handoff.astype(jnp.bfloat16)
    handoff = lax.all_to_all(handoff, "tensor", split_axis=1, concat_axis=0, tiled=True)
    handoff = lax.all_gather(handoff, "dp", axis=0, tiled=True)

    hidden = transposed_product(handoff, merge_weight).astype(jnp.bfloat16)
    hidden_block = hidden.shape[1]
    hidden = hidden.reshape(groups, image_count, hidden_block)
    placing = jnp.arange(groups * capacity, dtype=jnp.int32)[None, :, None] == target[:, None, :]
    placed = jnp.einsum(
        "spj,sjh->sph", placing.astype(jnp.bfloat16), hidden, preferred_element_type=jnp.float32
    ).astype(jnp.bfloat16)
    placed = placed.reshape(groups, groups, capacity, hidden_block).transpose(1, 0, 2, 3)
    placed = placed.reshape(groups, parts, groups * capacity // parts, hidden_block)
    summed = lax.psum_scatter(placed, "tensor", scatter_dimension=1, tiled=False)
    summed = lax.all_to_all(summed, "dp", split_axis=0, concat_axis=0, tiled=True)
    summed = summed.transpose(1, 0, 2).reshape(groups * capacity // parts, groups * hidden_block)
    hidden_grad = lax.all_to_all(summed, "tensor", split_axis=1, concat_axis=0, tiled=True)
    return hidden_grad.astype(jnp.float32) * gelu_slope(merge_pre)


Z = 4
CORES = 2
PARTS = 4
UNIT = 16
TILE = 128
MESH = pl.DeviceIdType.MESH
BF16 = jnp.bfloat16
F32 = jnp.float32


def stage_order(z, step):
    near = jnp.where(z >= 2, Z - 1 - z, z)
    at = jnp.where((near == 1) & (step < 2), 1 - step, step)
    return jnp.where(z >= 2, Z - 1 - at, at)


def remote(src, dst, send, recv, device):
    return pltpu.make_async_remote_copy(
        src_ref=src, dst_ref=dst, send_sem=send, recv_sem=recv, device_id=device, device_id_type=MESH
    )


def fused_kernel(
    capacity,
    gq, pos, count, dest, gain, wq_hbm, em_hbm, gr_hbm, wm_hbm, mp_hbm,
    out,
    wq, em, gr, wm, mp, slope, wq_t, wm_t,
    x, part, part_in, sums, grads,
    em_rows, gr_rows, ng, stat, rows_at,
    h, q, q_in, u, w, f,
    local_sem, x_s, x_r, part_s, part_r, sums_s, grads_r,
    ng_s, ng_r, stat_s, stat_r, at_s, at_r,
    h_s, h_r, q_s, q_r, u_s, w_r, w_s, f_r,
):
    s = lax.axis_index("dp")
    t = lax.axis_index("tensor")
    z = s // CORES
    c = s % CORES
    groups = Z * CORES
    sib = z * CORES + 1 - c
    sibling = (sib, t)
    tokens = gq.shape[0]
    image_count = pos.shape[1]
    half = image_count // 2
    rows = half // PARTS
    block = wq.shape[0]
    width = block * groups
    hidden = wm.shape[0]
    tiles = hidden // TILE
    pair_rows = CORES * capacity
    middle = (z == 1) | (z == 2)

    loads = [
        pltpu.make_async_copy(src, dst, local_sem.at[i])
        for i, (src, dst) in enumerate(
            ((wq_hbm, wq), (em_hbm, em), (gr_hbm, gr), (wm_hbm, wm), (mp_hbm, mp))
        )
    ]
    for load in loads:
        load.start()

    barrier = pltpu.get_barrier_semaphore()
    for k in range(1, groups):
        pl.semaphore_signal(barrier, inc=1, device_id=((s + k) % groups, t), device_id_type=MESH)
    for k in range(1, PARTS):
        pl.semaphore_signal(barrier, inc=1, device_id=(s, (t + k) % PARTS), device_id_type=MESH)

    hot = (lax.broadcasted_iota(jnp.int32, (tokens, image_count), 0) == pos[...]).astype(F32).astype(BF16)

    def pick(ref):
        return lax.dot_general(
            hot, ref[...], (((0,), (0,)), ((), ())), preferred_element_type=F32
        ).astype(BF16)

    x[pl.ds(s, 1)] = pick(gq).reshape(1, 2, half, -1)
    pl.semaphore_wait(barrier, groups - 1 + PARTS - 1)

    def kinds_of(ref, send, recv):
        def make(side, device):
            return lambda b, d: remote(
                ref.at[b, d], ref.at[b, d], send.at[b, d, side], recv.at[b, d], device
            )

        return make(0, (s + CORES, t)), make(1, (s - CORES, t)), make(2, sibling)

    x_kinds = kinds_of(x, x_s, x_r)
    h_kinds = kinds_of(h, h_s, h_r)

    def spread(act, kinds, zz, d):
        b = zz * CORES + c
        right, left, side = kinds

        @pl.when((zz <= z) & (z < Z - 1) & (c == 0))
        def _():
            act(right(b, d))

        @pl.when((zz >= z) & (z > 0))
        def _():
            act(left(b, d))

        @pl.when((zz <= z) & (z < Z - 1) & (c == 1))
        def _():
            act(right(b, d))

        act(side(b, d))

    def start(copy):
        copy.start()

    def sent(copy):
        copy.wait_send()

    def peer(k):
        return (t + k + c * (PARTS - 2 * k)) % PARTS

    def arrived(ref, sem):
        remote(ref, ref, x_s.at[0, 0, 0], sem, sibling).wait_recv()

    def pass_on(ref, recv, kinds, zz, d):
        b = zz * CORES + c
        arrived(ref.at[b, d], recv.at[b, d])
        spread(start, kinds, zz, d)

    spread(start, x_kinds, z, 0)

    lane = lax.broadcasted_iota(jnp.int32, (groups, image_count), 1)
    hot_dest = (dest[...] == lax.broadcasted_iota(jnp.int32, (groups, image_count), 0)) & (lane < count[0])
    hot_dest = hot_dest.astype(F32)
    before = (
        lax.broadcasted_iota(jnp.int32, (image_count, image_count), 0)
        < lax.broadcasted_iota(jnp.int32, (image_count, image_count), 1)
    ).astype(F32)
    earlier = jnp.dot(hot_dest, before, preferred_element_type=F32)
    slot = jnp.sum(earlier * hot_dest, axis=0, keepdims=True).astype(jnp.int32)
    spot = c * capacity + slot
    at = jnp.where(lane[:1] < count[0], dest[...] * pair_rows + spot, -1)
    rows_at[pl.ds(s, 1)] = jnp.broadcast_to(at, (1, 8, image_count))

    def at_copy(k):
        return remote(rows_at.at[s], rows_at.at[s], at_s.at[k], at_r.at[s], ((s + k) % groups, t))

    for k in range(1, groups):
        at_copy(k).start()

    def part_copy(d, zz, k):
        p = peer(k)
        return remote(
            part.at[d, zz, p], part_in.at[d, zz, t], part_s.at[d, zz, k], part_r.at[d, zz, t], (s, p)
        )

    def sums_copy(d, zz, cc):
        return remote(
            sums.at[d, zz, cc], grads.at[d, s], sums_s.at[d, zz, cc], grads_r.at[d, s],
            (zz * CORES + cc, t),
        )

    def add_parts(g):
        d = g // Z
        zz = stage_order(z, g % Z)
        total = part[d, zz, t].astype(F32)
        for k in range(1, PARTS):
            p = peer(k)
            arrived(part_in.at[d, zz, p], part_r.at[d, zz, p])
            total += part_in[d, zz, p].astype(F32)
        sums[pl.ds(d, 1), pl.ds(zz, 1)] = total.astype(BF16)[None, None]
        for cc in range(CORES):
            own = (zz == z) & (c == cc)

            @pl.when(jnp.logical_not(own))
            def _():
                sums_copy(d, zz, cc).start()

            @pl.when(own)
            def _():
                grads[pl.ds(d, 1), pl.ds(s, 1)] = sums[d, zz, cc][None, None]

    def grad_copy(d, k):
        p = peer(k)
        return remote(
            grads.at[d, pl.ds(p * 2, 2)], ng.at[d, t], ng_s.at[d, k], ng_r.at[d, t], (s, p)
        )

    def norm_send(d):
        for k in range(1, groups):
            b = (s + k) % groups
            arrived(grads.at[d, b], grads_r.at[d, b])
        for k in range(1, PARTS):
            grad_copy(d, k).start()
        ng[d, pl.ds(t, 1)] = grads[d, pl.ds(t * 2, 2)][None]

    def stat_copy(d, k):
        return remote(stat.at[d, t], stat.at[d, t], stat_s.at[d, k], stat_r.at[d, t], (s, peer(k)))

    def pieces(d, p):
        for e in range(2):
            lo = e * block
            top = d * half + p * rows
            value = em_rows[top:top + rows, lo:lo + block].astype(F32)
            yield lo, top, value, gain[:, lo:lo + block] * ng[d, p, e].astype(F32)

    def norm_stats(d):
        for k in range(1, PARTS):
            p = peer(k)
            arrived(ng.at[d, p], ng_r.at[d, p])
        side = lax.broadcasted_iota(jnp.int32, (rows, 128), 1)
        for p in range(PARTS):
            squares = jnp.zeros((rows, 1), F32)
            inner = jnp.zeros((rows, 1), F32)
            for lo, top, value, scaled in pieces(d, p):
                squares += jnp.sum(value * value, axis=1, keepdims=True)
                inner += jnp.sum(scaled * value, axis=1, keepdims=True)
            both = jnp.where(side < 64, squares, inner)
            stat[d, pl.ds(t, 1), p * rows:(p + 1) * rows] = both[None]
        for k in range(1, PARTS):
            stat_copy(d, k).start()

    def norm_finish(d):
        for k in range(1, PARTS):
            p = peer(k)
            arrived(stat.at[d, p], stat_r.at[d, p])
        for p in range(PARTS):
            total = jnp.zeros((rows, 128), F32)
            for src in range(PARTS):
                total += stat[d, src, p * rows:(p + 1) * rows]
            inverse = lax.rsqrt(total[:, 0:1] / width + NORM_EPS)
            back = inverse * inverse * inverse * total[:, 64:65] / width
            for lo, top, value, scaled in pieces(d, p):
                residual = gr_rows[top:top + rows, lo:lo + block].astype(F32)
                result = residual + inverse * scaled - value * back
                h[pl.ds(s, 1), d, p * rows:(p + 1) * rows, lo:lo + block] = result.astype(BF16)[None]
        spread(start, h_kinds, z, d)

    def turn(src, dst):
        for lo in range(0, src.shape[0], TILE):
            dst[:, lo:lo + TILE] = src[lo:lo + TILE].T

    loads[0].wait()
    turn(wq, wq_t)
    pass_on(x, x_r, x_kinds, stage_order(z, 1), 0)

    @pl.when(middle)
    def _():
        pass_on(x, x_r, x_kinds, stage_order(z, 2), 0)

    spread(start, x_kinds, z, 1)

    def first_step(g, carry):
        d, step = g // Z, g % Z
        zz = stage_order(z, step)
        passes = (g == Z + 1) | (step == 3) | ((step == 2) & jnp.logical_not(middle))
        late = (g == 2 * Z - 1) & jnp.logical_not(middle)

        @pl.when(passes & jnp.logical_not(late))
        def _():
            pass_on(x, x_r, x_kinds, zz, d)

        @pl.when((g == Z + 1) & middle)
        def _():
            pass_on(x, x_r, x_kinds, stage_order(z, 2), d)

        @pl.when(g == 2 * Z - 1)
        def _():
            norm_stats(0)

        @pl.when(late)
        def _():
            pass_on(x, x_r, x_kinds, zz, d)

        b = zz * CORES + 1 - c
        arrived(x.at[b, d], x_r.at[b, d])
        left = x[pl.ds(zz * CORES, CORES), pl.ds(d, 1)].reshape(CORES * half, -1)
        tile = 256
        for n in range(0, block, tile):
            piece = jnp.dot(left, wq_t[:, n:n + tile], preferred_element_type=F32).astype(BF16)
            piece = piece.reshape(CORES, PARTS, rows, tile)
            for p in range(PARTS):
                part[pl.ds(d, 1), pl.ds(zz, 1), p, :, :, n:n + tile] = piece[:, p][None, None]
        for k in range(1, PARTS):
            part_copy(d, zz, k).start()

        @pl.when(g == 1)
        def _():
            loads[1].wait()
            em_rows[...] = pick(em)
            loads[2].wait()
            gr_rows[...] = pick(gr)

        @pl.when(g == 2)
        def _():
            loads[3].wait()
            turn(wm, wm_t)

        @pl.when(g == 4)
        def _():
            loads[4].wait()

            def some_rows(i, carry):
                span = pl.ds(pl.multiple_of(i * UNIT, UNIT), UNIT)
                slope[span] = gelu_slope(mp[span])
                return carry

            lax.fori_loop(0, mp.shape[0] // UNIT, some_rows, 0)

        @pl.when(g == 2 * Z - 1)
        def _():
            norm_finish(0)

        @pl.when(g > 0)
        def _():
            add_parts(g - 1)

        @pl.when(g == 2 * Z - 2)
        def _():
            norm_send(0)

        return carry

    lax.fori_loop(0, 2 * Z, first_step, 0)
    add_parts(2 * Z - 1)

    pass_on(h, h_r, h_kinds, stage_order(z, 1), 0)

    @pl.when(middle)
    def _():
        pass_on(h, h_r, h_kinds, stage_order(z, 2), 0)

    norm_send(1)
    norm_stats(1)
    norm_finish(1)

    for k in range(1, groups):
        b = (s + k) % groups
        arrived(rows_at.at[b], at_r.at[b])

    def first_tile(zz):
        return (t + PARTS - zz) % PARTS

    def held(zz, e):
        return (first_tile(zz) == 0) | (e == 0)

    def tile_of(zz, e):
        return first_tile(zz) if e == 0 else PARTS

    def q_copy(zz, d, j):
        e = j // PARTS
        return remote(
            q.at[zz, d, j], q_in.at[zz, d, e, t], q_s.at[zz, d, j], q_r.at[zz, d, e, t],
            (s, (j + zz) % PARTS),
        )

    def u_copy(zz, e, r):
        return remote(u.at[zz, e, r], w.at[s, zz, e], u_s.at[zz, e, r], w_r.at[s, zz, e], (r, t))

    def add_tiles(zz):
        places = []
        for d in range(2):
            lo = d * half
            spots = jnp.concatenate(
                [rows_at[zz * CORES + cc, 0:1, lo:lo + half] for cc in range(CORES)], axis=1
            )
            hot_rows = lax.broadcasted_iota(jnp.int32, (groups * pair_rows, CORES * half), 0) == spots
            places.append(hot_rows.astype(F32).astype(BF16))
        for e in range(2):
            @pl.when(held(zz, e))
            def _():
                placed = jnp.zeros((groups * pair_rows, TILE), F32)
                for d in range(2):
                    total = q[zz, d, tile_of(zz, e)].astype(F32)
                    for k in range(1, PARTS):
                        p = peer(k)
                        arrived(q_in.at[zz, d, e, p], q_r.at[zz, d, e, p])
                        total += q_in[zz, d, e, p].astype(F32)
                    placed += jnp.dot(places[d], total.astype(BF16), preferred_element_type=F32)
                placed = placed.astype(BF16).reshape(1, 1, groups, pair_rows, TILE)
                u[pl.ds(zz, 1), e:e + 1] = placed
                for k in range(1, groups):
                    u_copy(zz, e, (s + k) % groups).start()
                w[pl.ds(s, 1), pl.ds(zz, 1), e] = u[zz, e, s][None, None]

    def f_copy(b, zz, e):
        j = tile_of(zz, e)
        return remote(
            w.at[b, zz, e], f.at[zz, b % 2, j], w_s.at[b, zz, e], f_r.at[zz, b % 2, j], (s, b // 2)
        )

    def hand_out(i, carry):
        step, k = i // groups, i % groups
        b = (s + k) % groups
        zz = stage_order(b // CORES, step)
        for e in range(2):
            @pl.when(held(zz, e))
            def _():
                @pl.when(b != s)
                def _():
                    arrived(w.at[b, zz, e], w_r.at[b, zz, e])

                @pl.when(b // 2 != t)
                def _():
                    f_copy(b, zz, e).start()

                @pl.when(b // 2 == t)
                def _():
                    f[pl.ds(zz, 1), pl.ds(b % 2, 1), pl.ds(tile_of(zz, e), 1)] = w[b, zz, e][None, None, None]

        return carry

    def first_sent(zz, carry):
        for d in range(2):
            spread(sent, x_kinds, zz, d)
            for k in range(1, PARTS):
                sent(part_copy(d, zz, k))
            for cc in range(CORES):
                @pl.when((zz != z) | (c != cc))
                def _():
                    sent(sums_copy(d, zz, cc))

        return carry

    def second_step(i, carry):
        step, d = i // 2, i % 2
        zz = stage_order(z, step)
        ends = jnp.logical_not(middle)

        @pl.when((i == 3) | ((i > 3) & ends))
        def _():
            pass_on(h, h_r, h_kinds, zz, d)

        @pl.when((i == 3) & middle)
        def _():
            pass_on(h, h_r, h_kinds, stage_order(z, 2), 1)

        b = zz * CORES + 1 - c
        arrived(h.at[b, d], h_r.at[b, d])
        left = h[pl.ds(zz * CORES, CORES), pl.ds(d, 1)].reshape(CORES * half, -1)
        for j in range(0, tiles, 2):
            hi = min(j + 2, tiles)
            piece = jnp.dot(left, wm_t[:, j * TILE:hi * TILE], preferred_element_type=F32).astype(BF16)
            for jj in range(j, hi):
                q[pl.ds(zz, 1), pl.ds(d, 1), jj] = piece[:, (jj - j) * TILE:(jj - j + 1) * TILE][None, None]
        for j in range(tiles):
            @pl.when((j + zz) % PARTS != t)
            def _():
                q_copy(zz, d, j).start()

        @pl.when(((i == 3) | (i == 5)) & middle)
        def _():
            pass_on(h, h_r, h_kinds, stage_order(z, 3), i // 5)

        @pl.when((i > 1) & (d == 0))
        def _():
            add_tiles(stage_order(z, step - 1))

        @pl.when(i == 6)
        def _():
            lax.fori_loop(0, 2 * groups, hand_out, 0)
            lax.fori_loop(0, Z, first_sent, 0)
            for k in range(1, groups):
                sent(at_copy(k))
            for d in range(2):
                for k in range(1, PARTS):
                    sent(grad_copy(d, k))
                    sent(stat_copy(d, k))


        return carry

    lax.fori_loop(0, 2 * Z, second_step, 0)
    add_tiles(stage_order(z, Z - 1))

    lax.fori_loop(2 * groups, Z * groups, hand_out, 0)

    def finish(zz, carry):
        span = pl.ds(pl.multiple_of(zz * pair_rows, pair_rows), pair_rows)
        for side in range(2):
            for j in range(tiles):
                @pl.when((j + zz) % PARTS != t)
                def _():
                    arrived(f.at[zz, side, j], f_r.at[zz, side, j])

                lo = side * hidden + j * TILE
                out[span, lo:lo + TILE] = f[zz, side, j].astype(F32) * slope[span, lo:lo + TILE]
        return carry

    lax.fori_loop(0, Z, finish, 0)

    def all_sent(zz, carry):
        for d in range(2):
            spread(sent, h_kinds, zz, d)

        for j in range(tiles):
            @pl.when((j + zz) % PARTS != t)
            def _():
                for d in range(2):
                    sent(q_copy(zz, d, j))

        for e in range(2):
            @pl.when(held(zz, e))
            def _():
                for k in range(1, groups):
                    sent(u_copy(zz, e, (s + k) % groups))
                for b in range(groups):
                    @pl.when(b // 2 != t)
                    def _():
                        sent(f_copy(b, zz, e))

        return carry

    lax.fori_loop(0, Z, all_sent, 0)


def fused(grad_query, query_weight, grad_resid, embeds, norm_gain, img_pos, img_count, img_dest, merge_weight, merge_pre):
    groups = Z * CORES
    capacity = merge_pre.shape[0] // groups
    image_count = img_pos.shape[1]
    half = image_count // 2
    rows = half // PARTS
    block, columns = query_weight.shape
    tiles = merge_weight.shape[0] // TILE
    pair_rows = CORES * capacity
    vmem = pltpu.VMEM
    dma = pltpu.SemaphoreType.DMA
    in_vmem = pl.BlockSpec(memory_space=pltpu.VMEM)
    anywhere = pl.BlockSpec(memory_space=pl.ANY)
    scratch = [
        vmem(query_weight.shape, BF16), vmem(embeds.shape, BF16), vmem(grad_resid.shape, BF16),
        vmem(merge_weight.shape, BF16), vmem(merge_pre.shape, BF16), vmem(merge_pre.shape, F32),
        vmem(query_weight.shape[::-1], BF16), vmem(merge_weight.shape[::-1], BF16),
        vmem((groups, 2, half, columns), BF16),
        vmem((2, Z, PARTS, CORES, rows, block), BF16), vmem((2, Z, PARTS, CORES, rows, block), BF16),
        vmem((2, Z, CORES, rows, block), BF16), vmem((2, groups, rows, block), BF16),
        vmem((image_count, columns), BF16), vmem((image_count, columns), BF16),
        vmem((2, PARTS, 2, rows, block), BF16), vmem((2, PARTS, half, 128), F32),
        vmem((groups, 8, image_count), jnp.int32),
        vmem((groups, 2, half, columns), BF16),
        vmem((Z, 2, tiles, CORES * half, TILE), BF16), vmem((Z, 2, 2, PARTS, CORES * half, TILE), BF16),
        vmem((Z, 2, groups, pair_rows, TILE), BF16), vmem((groups, Z, 2, pair_rows, TILE), BF16),
        vmem((Z, 2, tiles, pair_rows, TILE), BF16),
        dma((5,)), dma((groups, 2, 3)), dma((groups, 2)), dma((2, Z, PARTS)), dma((2, Z, PARTS)),
        dma((2, Z, CORES)), dma((2, groups)),
        dma((2, PARTS)), dma((2, PARTS)), dma((2, PARTS)), dma((2, PARTS)), dma((groups,)), dma((groups,)),
        dma((groups, 2, 3)), dma((groups, 2)), dma((Z, 2, tiles)), dma((Z, 2, 2, PARTS)),
        dma((Z, 2, groups)), dma((groups, Z, 2)), dma((groups, Z, 2)), dma((Z, 2, tiles)),
    ]
    return pl.pallas_call(
        functools.partial(fused_kernel, capacity),
        out_shape=jax.ShapeDtypeStruct(merge_pre.shape, F32),
        in_specs=[
            in_vmem, in_vmem, pl.BlockSpec(memory_space=pltpu.SMEM), in_vmem, in_vmem,
            anywhere, anywhere, anywhere, anywhere, anywhere,
        ],
        out_specs=in_vmem,
        scratch_shapes=scratch,
        compiler_params=pltpu.CompilerParams(
            collective_id=0, has_side_effects=True, vmem_limit_bytes=56 * 1024 * 1024
        ),
        cost_estimate=pl.CostEstimate(
            flops=4 * groups * image_count * columns * (block + merge_weight.shape[0]),
            bytes_accessed=16 * 1024 * 1024,
            transcendentals=merge_pre.size,
        ),
    )(
        grad_query, img_pos, img_count, img_dest, norm_gain.reshape(1, -1),
        query_weight, embeds, grad_resid, merge_weight, merge_pre,
    )


def solution(mesh):
    in_specs = (
        P("dp", "tensor"),
        P("dp", "tensor"),
        P("dp", "tensor"),
        P("dp", "tensor"),
        P("tensor"),
        P("dp", None),
        P("dp"),
        P("dp", None),
        P("dp", "tensor"),
        P("dp", "tensor"),
    )
    out_specs = P("dp", "tensor")
    known = mesh.shape["dp"] == Z * CORES and mesh.shape["tensor"] == PARTS
    body = fused if known else local
    return jax.shard_map(body, mesh=mesh, in_specs=in_specs, out_specs=out_specs, check_vma=False)
```

```python
import functools

import jax
import jax.numpy as jnp
from jax import lax
from jax.experimental import pallas as pl
from jax.experimental.pallas import tpu as pltpu
from jax.sharding import PartitionSpec as P

NORM_EPS = 1e-06


def gelu_slope(pre):
    value = pre.astype(jnp.float32)
    cdf_part = 0.5 * (1.0 + lax.erf(value * 0.7071067811865476))
    pdf_part = jnp.exp(-0.5 * value * value) * 0.3989422804014327
    return cdf_part + value * pdf_part


def transposed_product(left, right):
    return lax.dot_general(
        left, right, (((1,), (1,)), ((), ())), preferred_element_type=jnp.float32
    )


def targets(img_count, img_dest, groups, capacity):
    image_count = img_dest.shape[1]
    is_live = jnp.arange(image_count, dtype=jnp.int32) < img_count[0]
    target_dev = img_dest[0]
    dest_hot = (
        (target_dev[:, None] == jnp.arange(groups, dtype=jnp.int32)[None, :]) & is_live[:, None]
    ).astype(jnp.int32)
    earlier = jnp.cumsum(dest_hot, axis=0) - dest_hot
    slot_index = jnp.sum(earlier * dest_hot, axis=1)
    return jnp.where(is_live, target_dev * capacity + slot_index, -1)


def local(
    grad_query,
    query_weight,
    grad_resid,
    embeds,
    norm_gain,
    img_pos,
    img_count,
    img_dest,
    merge_weight,
    merge_pre,
):
    groups = lax.axis_size("dp")
    parts = lax.axis_size("tensor")
    capacity = merge_pre.shape[0] // groups
    positions = img_pos[0]
    image_count = positions.shape[0]
    rows = image_count // parts
    block = query_weight.shape[0]
    width = block * groups
    picked = lax.all_gather(jnp.take(grad_query, positions, axis=0), "dp", axis=0, tiled=True)
    inputs = jnp.take(embeds, positions, axis=0)
    residual = jnp.take(grad_resid, positions, axis=0)
    inputs = lax.all_to_all(inputs, "tensor", split_axis=0, concat_axis=1, tiled=True)
    residual = lax.all_to_all(residual, "tensor", split_axis=0, concat_axis=1, tiled=True)
    inputs = inputs.astype(jnp.float32)
    gain = lax.all_gather(norm_gain, "tensor", axis=0, tiled=True)
    target = targets(img_count, img_dest, groups, capacity)
    target = lax.all_gather(target, "dp", axis=0)

    partial_value = transposed_product(picked, query_weight).astype(jnp.bfloat16)
    partial_value = partial_value.reshape(groups, parts, rows, block)
    summed = lax.psum_scatter(partial_value, "tensor", scatter_dimension=1, tiled=False)
    normal_grad = lax.all_to_all(summed, "dp", split_axis=0, concat_axis=0, tiled=True)
    normal_grad = normal_grad.transpose(1, 0, 2).reshape(rows, width).astype(jnp.float32)

    scaled = gain[None, :] * normal_grad
    squares = jnp.sum(inputs * inputs, axis=1)
    inner_sum = jnp.sum(scaled * inputs, axis=1)
    inverse = lax.rsqrt(squares / width + NORM_EPS)
    handoff = (
        residual.astype(jnp.float32)
        + inverse[:, None] * scaled
        - inputs * (inverse**3 * inner_sum / width)[:, None]
    )
    handoff = handoff.astype(jnp.bfloat16)
    handoff = lax.all_to_all(handoff, "tensor", split_axis=1, concat_axis=0, tiled=True)
    handoff = lax.all_gather(handoff, "dp", axis=0, tiled=True)

    hidden = transposed_product(handoff, merge_weight).astype(jnp.bfloat16)
    hidden_block = hidden.shape[1]
    hidden = hidden.reshape(groups, image_count, hidden_block)
    placing = jnp.arange(groups * capacity, dtype=jnp.int32)[None, :, None] == target[:, None, :]
    placed = jnp.einsum(
        "spj,sjh->sph", placing.astype(jnp.bfloat16), hidden, preferred_element_type=jnp.float32
    ).astype(jnp.bfloat16)
    placed = placed.reshape(groups, groups, capacity, hidden_block).transpose(1, 0, 2, 3)
    placed = placed.reshape(groups, parts, groups * capacity // parts, hidden_block)
    summed = lax.psum_scatter(placed, "tensor", scatter_dimension=1, tiled=False)
    summed = lax.all_to_all(summed, "dp", split_axis=0, concat_axis=0, tiled=True)
    summed = summed.transpose(1, 0, 2).reshape(groups * capacity // parts, groups * hidden_block)
    hidden_grad = lax.all_to_all(summed, "tensor", split_axis=1, concat_axis=0, tiled=True)
    return hidden_grad.astype(jnp.float32) * gelu_slope(merge_pre)


Z = 4
CORES = 2
PARTS = 4
UNIT = 16
TILE = 128
MESH = pl.DeviceIdType.MESH
BF16 = jnp.bfloat16
F32 = jnp.float32


def stage_order(z, step):
    near = jnp.where(z >= 2, Z - 1 - z, z)
    at = jnp.where((near == 1) & (step < 2), 1 - step, step)
    return jnp.where(z >= 2, Z - 1 - at, at)


def remote(src, dst, send, recv, device):
    return pltpu.make_async_remote_copy(
        src_ref=src, dst_ref=dst, send_sem=send, recv_sem=recv, device_id=device, device_id_type=MESH
    )


def fused_kernel(
    capacity,
    gq, pos, count, dest, gain, wq_hbm, em_hbm, gr_hbm, wm_hbm,
    out,
    wq, em, gr, wm,
    x, part, part_in, sums, grads,
    em_rows, gr_rows, ng, stat, rows_at,
    h, q, q_in, u, w, f,
    local_sem, x_s, x_r, part_s, part_r, sums_s, grads_r,
    ng_s, ng_r, stat_s, stat_r, at_s, at_r,
    h_s, h_r, q_s, q_r, u_s, w_r, w_s, f_r,
):
    s = lax.axis_index("dp")
    t = lax.axis_index("tensor")
    z = s // CORES
    c = s % CORES
    groups = Z * CORES
    sib = z * CORES + 1 - c
    sibling = (sib, t)
    tokens = gq.shape[0]
    image_count = pos.shape[1]
    half = image_count // 2
    rows = half // PARTS
    block = wq.shape[0]
    width = block * groups
    hidden = wm.shape[0]
    tiles = hidden // TILE
    pair_rows = CORES * capacity
    middle = (z == 1) | (z == 2)

    loads = [
        pltpu.make_async_copy(src, dst, local_sem.at[i])
        for i, (src, dst) in enumerate(
            ((wq_hbm, wq), (em_hbm, em), (gr_hbm, gr), (wm_hbm, wm))
        )
    ]
    for load in loads:
        load.start()

    barrier = pltpu.get_barrier_semaphore()
    for k in range(1, groups):
        pl.semaphore_signal(barrier, inc=1, device_id=((s + k) % groups, t), device_id_type=MESH)
    for k in range(1, PARTS):
        pl.semaphore_signal(barrier, inc=1, device_id=(s, (t + k) % PARTS), device_id_type=MESH)

    hot = (lax.broadcasted_iota(jnp.int32, (tokens, image_count), 0) == pos[...]).astype(F32).astype(BF16)

    def pick(ref):
        return lax.dot_general(
            hot, ref[...], (((0,), (0,)), ((), ())), preferred_element_type=F32
        ).astype(BF16)

    x[pl.ds(s, 1)] = pick(gq).reshape(1, 2, half, -1)
    pl.semaphore_wait(barrier, groups - 1 + PARTS - 1)

    def kinds_of(ref, send, recv):
        def make(side, device):
            return lambda b, d: remote(
                ref.at[b, d], ref.at[b, d], send.at[b, d, side], recv.at[b, d], device
            )

        return make(0, (s + CORES, t)), make(1, (s - CORES, t)), make(2, sibling)

    x_kinds = kinds_of(x, x_s, x_r)
    h_kinds = kinds_of(h, h_s, h_r)

    def spread(act, kinds, zz, d):
        b = zz * CORES + c
        right, left, side = kinds

        @pl.when((zz <= z) & (z < Z - 1) & (c == 0))
        def _():
            act(right(b, d))

        @pl.when((zz >= z) & (z > 0))
        def _():
            act(left(b, d))

        @pl.when((zz <= z) & (z < Z - 1) & (c == 1))
        def _():
            act(right(b, d))

        act(side(b, d))

    def start(copy):
        copy.start()

    def sent(copy):
        copy.wait_send()

    def peer(k):
        return (t + k + c * (PARTS - 2 * k)) % PARTS

    def arrived(ref, sem):
        remote(ref, ref, x_s.at[0, 0, 0], sem, sibling).wait_recv()

    def pass_on(ref, recv, kinds, zz, d):
        b = zz * CORES + c
        arrived(ref.at[b, d], recv.at[b, d])
        spread(start, kinds, zz, d)

    spread(start, x_kinds, z, 0)

    lane = lax.broadcasted_iota(jnp.int32, (groups, image_count), 1)
    hot_dest = (dest[...] == lax.broadcasted_iota(jnp.int32, (groups, image_count), 0)) & (lane < count[0])
    hot_dest = hot_dest.astype(F32)
    before = (
        lax.broadcasted_iota(jnp.int32, (image_count, image_count), 0)
        < lax.broadcasted_iota(jnp.int32, (image_count, image_count), 1)
    ).astype(F32)
    earlier = jnp.dot(hot_dest, before, preferred_element_type=F32)
    slot = jnp.sum(earlier * hot_dest, axis=0, keepdims=True).astype(jnp.int32)
    spot = c * capacity + slot
    at = jnp.where(lane[:1] < count[0], dest[...] * pair_rows + spot, -1)
    rows_at[pl.ds(s, 1)] = jnp.broadcast_to(at, (1, 8, image_count))

    def at_copy(k):
        return remote(rows_at.at[s], rows_at.at[s], at_s.at[k], at_r.at[s], ((s + k) % groups, t))

    for k in range(1, groups):
        at_copy(k).start()

    def part_copy(d, zz, k):
        p = peer(k)
        return remote(
            part.at[d, zz, p], part_in.at[d, zz, t], part_s.at[d, zz, k], part_r.at[d, zz, t], (s, p)
        )

    def sums_copy(d, zz, cc):
        return remote(
            sums.at[d, zz, cc], grads.at[d, s], sums_s.at[d, zz, cc], grads_r.at[d, s],
            (zz * CORES + cc, t),
        )

    def add_parts(g):
        d = g // Z
        zz = stage_order(z, g % Z)
        total = part[d, zz, t].astype(F32)
        for k in range(1, PARTS):
            p = peer(k)
            arrived(part_in.at[d, zz, p], part_r.at[d, zz, p])
            total += part_in[d, zz, p].astype(F32)
        sums[pl.ds(d, 1), pl.ds(zz, 1)] = total.astype(BF16)[None, None]
        for cc in range(CORES):
            own = (zz == z) & (c == cc)

            @pl.when(jnp.logical_not(own))
            def _():
                sums_copy(d, zz, cc).start()

            @pl.when(own)
            def _():
                grads[pl.ds(d, 1), pl.ds(s, 1)] = sums[d, zz, cc][None, None]

    def grad_copy(d, k):
        p = peer(k)
        return remote(
            grads.at[d, pl.ds(p * 2, 2)], ng.at[d, t], ng_s.at[d, k], ng_r.at[d, t], (s, p)
        )

    def norm_send(d):
        for k in range(1, groups):
            b = (s + k) % groups
            arrived(grads.at[d, b], grads_r.at[d, b])
        for k in range(1, PARTS):
            grad_copy(d, k).start()
        ng[d, pl.ds(t, 1)] = grads[d, pl.ds(t * 2, 2)][None]

    def stat_copy(d, k):
        return remote(stat.at[d, t], stat.at[d, t], stat_s.at[d, k], stat_r.at[d, t], (s, peer(k)))

    def pieces(d, p):
        for e in range(2):
            lo = e * block
            top = d * half + p * rows
            value = em_rows[top:top + rows, lo:lo + block].astype(F32)
            yield lo, top, value, gain[:, lo:lo + block] * ng[d, p, e].astype(F32)

    def norm_stats(d):
        for k in range(1, PARTS):
            p = peer(k)
            arrived(ng.at[d, p], ng_r.at[d, p])
        side = lax.broadcasted_iota(jnp.int32, (rows, 128), 1)
        for p in range(PARTS):
            squares = jnp.zeros((rows, 1), F32)
            inner = jnp.zeros((rows, 1), F32)
            for lo, top, value, scaled in pieces(d, p):
                squares += jnp.sum(value * value, axis=1, keepdims=True)
                inner += jnp.sum(scaled * value, axis=1, keepdims=True)
            both = jnp.where(side < 64, squares, inner)
            stat[d, pl.ds(t, 1), p * rows:(p + 1) * rows] = both[None]
        for k in range(1, PARTS):
            stat_copy(d, k).start()

    def norm_finish(d):
        for k in range(1, PARTS):
            p = peer(k)
            arrived(stat.at[d, p], stat_r.at[d, p])
        for p in range(PARTS):
            total = jnp.zeros((rows, 128), F32)
            for src in range(PARTS):
                total += stat[d, src, p * rows:(p + 1) * rows]
            inverse = lax.rsqrt(total[:, 0:1] / width + NORM_EPS)
            back = inverse * inverse * inverse * total[:, 64:65] / width
            for lo, top, value, scaled in pieces(d, p):
                residual = gr_rows[top:top + rows, lo:lo + block].astype(F32)
                result = residual + inverse * scaled - value * back
                h[pl.ds(s, 1), d, p * rows:(p + 1) * rows, lo:lo + block] = result.astype(BF16)[None]
        spread(start, h_kinds, z, d)

    loads[0].wait()
    pass_on(x, x_r, x_kinds, stage_order(z, 1), 0)

    @pl.when(middle)
    def _():
        pass_on(x, x_r, x_kinds, stage_order(z, 2), 0)

    spread(start, x_kinds, z, 1)

    def first_step(g, carry):
        d, step = g // Z, g % Z
        zz = stage_order(z, step)
        passes = (g == Z + 1) | (step == 3) | ((step == 2) & jnp.logical_not(middle))
        late = (g == 2 * Z - 1) & jnp.logical_not(middle)

        @pl.when(passes & jnp.logical_not(late))
        def _():
            pass_on(x, x_r, x_kinds, zz, d)

        @pl.when((g == Z + 1) & middle)
        def _():
            pass_on(x, x_r, x_kinds, stage_order(z, 2), d)

        @pl.when(g == 2 * Z - 1)
        def _():
            norm_stats(0)

        @pl.when(late)
        def _():
            pass_on(x, x_r, x_kinds, zz, d)

        b = zz * CORES + 1 - c
        arrived(x.at[b, d], x_r.at[b, d])
        left = x[pl.ds(zz * CORES, CORES), pl.ds(d, 1)].reshape(CORES * half, -1)
        tile = 256
        for n in range(0, block, tile):
            piece = transposed_product(left, wq[n:n + tile]).astype(BF16)
            piece = piece.reshape(CORES, PARTS, rows, tile)
            for p in range(PARTS):
                part[pl.ds(d, 1), pl.ds(zz, 1), p, :, :, n:n + tile] = piece[:, p][None, None]
        for k in range(1, PARTS):
            part_copy(d, zz, k).start()

        @pl.when(g == 1)
        def _():
            loads[1].wait()
            em_rows[...] = pick(em)
            loads[2].wait()
            gr_rows[...] = pick(gr)

        @pl.when(g == 2 * Z - 1)
        def _():
            norm_finish(0)

        @pl.when(g > 0)
        def _():
            add_parts(g - 1)

        @pl.when(g == 2 * Z - 2)
        def _():
            norm_send(0)

        return carry

    lax.fori_loop(0, 2 * Z, first_step, 0)
    add_parts(2 * Z - 1)

    pass_on(h, h_r, h_kinds, stage_order(z, 1), 0)

    @pl.when(middle)
    def _():
        pass_on(h, h_r, h_kinds, stage_order(z, 2), 0)

    norm_send(1)
    norm_stats(1)
    norm_finish(1)

    for k in range(1, groups):
        b = (s + k) % groups
        arrived(rows_at.at[b], at_r.at[b])
    loads[3].wait()

    def first_tile(zz):
        return (t + PARTS - zz) % PARTS

    def held(zz, e):
        return (first_tile(zz) == 0) | (e == 0)

    def tile_of(zz, e):
        return first_tile(zz) if e == 0 else PARTS

    def q_copy(zz, d, j):
        e = j // PARTS
        return remote(
            q.at[zz, d, j], q_in.at[zz, d, e, t], q_s.at[zz, d, j], q_r.at[zz, d, e, t],
            (s, (j + zz) % PARTS),
        )

    def u_copy(zz, e, r):
        return remote(u.at[zz, e, r], w.at[s, zz, e], u_s.at[zz, e, r], w_r.at[s, zz, e], (r, t))

    def add_tiles(zz):
        places = []
        for d in range(2):
            lo = d * half
            spots = jnp.concatenate(
                [rows_at[zz * CORES + cc, 0:1, lo:lo + half] for cc in range(CORES)], axis=1
            )
            hot_rows = lax.broadcasted_iota(jnp.int32, (groups * pair_rows, CORES * half), 0) == spots
            places.append(hot_rows.astype(F32).astype(BF16))
        for e in range(2):
            @pl.when(held(zz, e))
            def _():
                placed = jnp.zeros((groups * pair_rows, TILE), F32)
                for d in range(2):
                    total = q[zz, d, tile_of(zz, e)].astype(F32)
                    for k in range(1, PARTS):
                        p = peer(k)
                        arrived(q_in.at[zz, d, e, p], q_r.at[zz, d, e, p])
                        total += q_in[zz, d, e, p].astype(F32)
                    placed += jnp.dot(places[d], total.astype(BF16), preferred_element_type=F32)
                placed = placed.astype(BF16).reshape(1, 1, groups, pair_rows, TILE)
                u[pl.ds(zz, 1), e:e + 1] = placed
                for k in range(1, groups):
                    u_copy(zz, e, (s + k) % groups).start()
                w[pl.ds(s, 1), pl.ds(zz, 1), e] = u[zz, e, s][None, None]

    def f_copy(b, zz, e):
        j = tile_of(zz, e)
        return remote(
            w.at[b, zz, e], f.at[zz, b % 2, j], w_s.at[b, zz, e], f_r.at[zz, b % 2, j], (s, b // 2)
        )

    def hand_out(i, carry):
        step, k = i // groups, i % groups
        b = (s + k) % groups
        zz = stage_order(b // CORES, step)
        for e in range(2):
            @pl.when(held(zz, e))
            def _():
                @pl.when(b != s)
                def _():
                    arrived(w.at[b, zz, e], w_r.at[b, zz, e])

                @pl.when(b // 2 != t)
                def _():
                    f_copy(b, zz, e).start()

                @pl.when(b // 2 == t)
                def _():
                    f[pl.ds(zz, 1), pl.ds(b % 2, 1), pl.ds(tile_of(zz, e), 1)] = w[b, zz, e][None, None, None]

        return carry

    def first_sent(zz, carry):
        for d in range(2):
            spread(sent, x_kinds, zz, d)
            for k in range(1, PARTS):
                sent(part_copy(d, zz, k))
            for cc in range(CORES):
                @pl.when((zz != z) | (c != cc))
                def _():
                    sent(sums_copy(d, zz, cc))

        return carry

    def second_step(i, carry):
        step, d = i // 2, i % 2
        zz = stage_order(z, step)
        ends = jnp.logical_not(middle)

        @pl.when((i == 3) | ((i > 3) & ends))
        def _():
            pass_on(h, h_r, h_kinds, zz, d)

        @pl.when((i == 3) & middle)
        def _():
            pass_on(h, h_r, h_kinds, stage_order(z, 2), 1)

        b = zz * CORES + 1 - c
        arrived(h.at[b, d], h_r.at[b, d])
        left = h[pl.ds(zz * CORES, CORES), pl.ds(d, 1)].reshape(CORES * half, -1)
        for j in range(0, tiles, 2):
            hi = min(j + 2, tiles)
            piece = transposed_product(left, wm[j * TILE:hi * TILE]).astype(BF16)
            for jj in range(j, hi):
                q[pl.ds(zz, 1), pl.ds(d, 1), jj] = piece[:, (jj - j) * TILE:(jj - j + 1) * TILE][None, None]
        for j in range(tiles):
            @pl.when((j + zz) % PARTS != t)
            def _():
                q_copy(zz, d, j).start()

        @pl.when(((i == 3) | (i == 5)) & middle)
        def _():
            pass_on(h, h_r, h_kinds, stage_order(z, 3), i // 5)

        @pl.when((i > 1) & (d == 0))
        def _():
            add_tiles(stage_order(z, step - 1))

        @pl.when(i == 6)
        def _():
            lax.fori_loop(0, 2 * groups, hand_out, 0)
            lax.fori_loop(0, Z, first_sent, 0)
            for k in range(1, groups):
                sent(at_copy(k))
            for d in range(2):
                for k in range(1, PARTS):
                    sent(grad_copy(d, k))
                    sent(stat_copy(d, k))


        return carry

    lax.fori_loop(0, 2 * Z, second_step, 0)
    add_tiles(stage_order(z, Z - 1))

    lax.fori_loop(2 * groups, Z * groups, hand_out, 0)

    def finish(zz, carry):
        span = pl.ds(pl.multiple_of(zz * pair_rows, pair_rows), pair_rows)
        for side in range(2):
            for j in range(tiles):
                @pl.when((j + zz) % PARTS != t)
                def _():
                    arrived(f.at[zz, side, j], f_r.at[zz, side, j])

                lo = side * hidden + j * TILE
                out[span, lo:lo + TILE] = f[zz, side, j]
        return carry

    lax.fori_loop(0, Z, finish, 0)

    def all_sent(zz, carry):
        for d in range(2):
            spread(sent, h_kinds, zz, d)

        for j in range(tiles):
            @pl.when((j + zz) % PARTS != t)
            def _():
                for d in range(2):
                    sent(q_copy(zz, d, j))

        for e in range(2):
            @pl.when(held(zz, e))
            def _():
                for k in range(1, groups):
                    sent(u_copy(zz, e, (s + k) % groups))
                for b in range(groups):
                    @pl.when(b // 2 != t)
                    def _():
                        sent(f_copy(b, zz, e))

        return carry

    lax.fori_loop(0, Z, all_sent, 0)


def fused(grad_query, query_weight, grad_resid, embeds, norm_gain, img_pos, img_count, img_dest, merge_weight, merge_pre):
    groups = Z * CORES
    capacity = merge_pre.shape[0] // groups
    image_count = img_pos.shape[1]
    half = image_count // 2
    rows = half // PARTS
    block, columns = query_weight.shape
    tiles = merge_weight.shape[0] // TILE
    pair_rows = CORES * capacity
    vmem = pltpu.VMEM
    dma = pltpu.SemaphoreType.DMA
    in_vmem = pl.BlockSpec(memory_space=pltpu.VMEM)
    anywhere = pl.BlockSpec(memory_space=pl.ANY)
    scratch = [
        vmem(query_weight.shape, BF16), vmem(embeds.shape, BF16), vmem(grad_resid.shape, BF16),
        vmem(merge_weight.shape, BF16),
        vmem((groups, 2, half, columns), BF16),
        vmem((2, Z, PARTS, CORES, rows, block), BF16), vmem((2, Z, PARTS, CORES, rows, block), BF16),
        vmem((2, Z, CORES, rows, block), BF16), vmem((2, groups, rows, block), BF16),
        vmem((image_count, columns), BF16), vmem((image_count, columns), BF16),
        vmem((2, PARTS, 2, rows, block), BF16), vmem((2, PARTS, half, 128), F32),
        vmem((groups, 8, image_count), jnp.int32),
        vmem((groups, 2, half, columns), BF16),
        vmem((Z, 2, tiles, CORES * half, TILE), BF16), vmem((Z, 2, 2, PARTS, CORES * half, TILE), BF16),
        vmem((Z, 2, groups, pair_rows, TILE), BF16), vmem((groups, Z, 2, pair_rows, TILE), BF16),
        vmem((Z, 2, tiles, pair_rows, TILE), BF16),
        dma((5,)), dma((groups, 2, 3)), dma((groups, 2)), dma((2, Z, PARTS)), dma((2, Z, PARTS)),
        dma((2, Z, CORES)), dma((2, groups)),
        dma((2, PARTS)), dma((2, PARTS)), dma((2, PARTS)), dma((2, PARTS)), dma((groups,)), dma((groups,)),
        dma((groups, 2, 3)), dma((groups, 2)), dma((Z, 2, tiles)), dma((Z, 2, 2, PARTS)),
        dma((Z, 2, groups)), dma((groups, Z, 2)), dma((groups, Z, 2)), dma((Z, 2, tiles)),
    ]
    hidden_grad = pl.pallas_call(
        functools.partial(fused_kernel, capacity),
        out_shape=jax.ShapeDtypeStruct(merge_pre.shape, BF16),
        in_specs=[
            in_vmem, in_vmem, pl.BlockSpec(memory_space=pltpu.SMEM), in_vmem, in_vmem,
            anywhere, anywhere, anywhere, anywhere,
        ],
        out_specs=in_vmem,
        scratch_shapes=scratch,
        compiler_params=pltpu.CompilerParams(
            collective_id=0, has_side_effects=True, vmem_limit_bytes=56 * 1024 * 1024
        ),
        cost_estimate=pl.CostEstimate(
            flops=4 * groups * image_count * columns * (block + merge_weight.shape[0]),
            bytes_accessed=16 * 1024 * 1024,
            transcendentals=0,
        ),
    )(
        grad_query, img_pos, img_count, img_dest, norm_gain.reshape(1, -1),
        query_weight, embeds, grad_resid, merge_weight,
    )
    return hidden_grad.astype(F32) * gelu_slope(merge_pre)


def solution(mesh):
    in_specs = (
        P("dp", "tensor"),
        P("dp", "tensor"),
        P("dp", "tensor"),
        P("dp", "tensor"),
        P("tensor"),
        P("dp", None),
        P("dp"),
        P("dp", None),
        P("dp", "tensor"),
        P("dp", "tensor"),
    )
    out_specs = P("dp", "tensor")
    known = mesh.shape["dp"] == Z * CORES and mesh.shape["tensor"] == PARTS
    body = fused if known else local
    return jax.shard_map(body, mesh=mesh, in_specs=in_specs, out_specs=out_specs, check_vma=False)
```
